128 devices in a mesh: slab: 32 (over z, x, core), bal: 4 (over y).
Axes of the slice: x: 4, y: 4, z: 4, core: 2. Of those that a mesh axis runs over, the one named last changes fastest.
Arguments:
- volume: bfloat16 [128, 4, 64, 4096], P(('slab', 'bal')), may hold values from -150 to 150
- first_kernel: bfloat16 [3, 3, 3, 32], replicated, may hold values from -1.25 to 1.25
- second_kernel: bfloat16 [3, 3, 3, 32, 32], replicated, may hold values from -0.21875 to 0.21875
- class_weights: bfloat16 [32, 3], replicated, may hold values from -40 to 40
- patch_corners: int32 [128, 6, 3], P(('slab', 'bal')), may hold values from 0 to 127, as said below
- patch_counts: int32 [128], replicated, may hold values from 0 to 6, as said below
Outputs:
- probabilities: float32 [128, 4, 64, 3, 4096], P(('slab', 'bal'))
The draws below stay inside these ranges and needn't reach their ends.
Inputs may be any that keep to these rules, and one draw needn't show every extreme that they name: `patch_corners`: entry x of every corner equals its column's index; for tissue patches x + 1 < 128; y <= 2 and z <= 62. The entries of one column's list are different corners; entries past patch_counts are listed corners that are not tissue patches. `patch_counts`: the last column has none; every other column has at least one. In every group of 4 consecutive columns one column has exactly 6; the columns of a group hold at most 12 together, and some group exactly that many.
All inputs are finite; a program needn't handle non-finite values.
Results may differ from the reference program's by a relative error of at most 0.0086.
Values may be sent and summed in bfloat16 or wider, within the bound.
No kernel may reach another device: no remote copies, remote signals or barrier semaphores. Data moves between devices by JAX's collectives and lax.ppermute only.
A program may use at most 128 MiB of HBM per device.

```python
import math
import jax
import jax.numpy as jnp
from jax import lax

PATCH = 32
HALF = 16
TILE_VOX = 4096
CHANNELS = 32
CLASSES = 3
TILES_Y = 4
TILES_Z = 64
HOME_MOST = 6
TILES_X = 128
WORK_MOST = 3
N_BAL = 4


def layout(key):
    groups = TILES_X // N_BAL
    subkeys = jax.random.split(key, 5)
    group_ids = jnp.arange(groups)
    heavy_home = jax.random.randint(subkeys[0], (groups,), 0, N_BAL)
    heavy_home = jnp.where(group_ids == groups - 1, heavy_home % (N_BAL - 1), heavy_home)
    filled = jax.random.randint(subkeys[1], (), 0, groups - 1)
    shortfall = jax.random.randint(subkeys[2], (groups,), 0, 2)
    shortfall = jnp.where(group_ids == filled, 0, shortfall)
    spare_units = N_BAL * WORK_MOST - HOME_MOST - shortfall - (N_BAL - 1)
    owners = jax.random.randint(subkeys[3], (groups, HOME_MOST), 0, N_BAL - 1)
    active = jnp.arange(HOME_MOST)[None, :] < spare_units[:, None]
    matches = (owners[:, :, None] == jnp.arange(N_BAL - 1)[None, None, :]) & active[:, :, None]
    others = 1 + jnp.sum(matches.astype(jnp.int32), axis=1)
    member = jnp.arange(N_BAL)[None, :]
    other_pos = jnp.clip(member - (member > heavy_home[:, None]).astype(jnp.int32), 0, N_BAL - 2)
    counts = jnp.where(member == heavy_home[:, None], HOME_MOST, jnp.take_along_axis(others, other_pos, axis=1))
    last_home = (group_ids[:, None] == groups - 1) & (member == N_BAL - 1)
    counts = jnp.where(last_home, 0, counts).astype(jnp.int32)
    places = (TILES_Y - 1) * (TILES_Z - 1)
    column_keys = jax.random.split(subkeys[4], TILES_X)
    shuffled = jax.vmap(lambda single: jax.random.permutation(single, places))(column_keys)[:, :HOME_MOST]
    columns = jnp.broadcast_to(jnp.arange(TILES_X)[:, None], (TILES_X, HOME_MOST))
    corners = jnp.stack([columns, shuffled // (TILES_Z - 1), shuffled % (TILES_Z - 1)], axis=2).astype(jnp.int32)
    return (corners, counts.reshape(TILES_X))


def draw_patch_corners(key, part):
    shared = layout(key)
    return shared[0]


def draw_patch_counts(key, part):
    shared = layout(key)
    return shared[1]


def draw_volume(key, part):
    key = jax.random.fold_in(key, 7)
    subkeys = jax.random.split(key, 3)
    full_shape = (TILES_X, TILES_Y, TILES_Z, TILE_VOX)
    tile_scale = jnp.exp(jax.random.uniform(subkeys[0], (TILES_X, TILES_Y, TILES_Z, 1), jnp.float32) * math.log(3.0))
    voxel_scale = jnp.exp(jax.random.uniform(subkeys[1], full_shape, jnp.float32) * math.log(10.0))
    field_out = jax.random.normal(subkeys[2], full_shape, jnp.float32) * voxel_scale * tile_scale
    return jnp.clip(field_out, -150.0, 150.0).astype(jnp.bfloat16)


def draw_class_weights(key, part):
    key = jax.random.fold_in(key, 9)
    subkeys = jax.random.split(key, 1)
    scale_in = CHANNELS ** (-0.5)
    table = jax.random.normal(subkeys[0], (CHANNELS, CLASSES), jnp.float32) * (3.0 * scale_in)
    return jnp.clip(table, -40.0, 40.0).astype(jnp.bfloat16)


def bell_draw(stream_key, dims, scale, limit, kind=jnp.bfloat16):
    array = scale * jax.random.normal(stream_key, dims, jnp.float32)
    return jnp.clip(array, min=-limit, max=limit).astype(kind)


def setup_inputs(seed: int = 0) -> dict:
    arg_keys = jax.random.split(jax.random.key(seed), 7)
    return {
        "volume": draw_volume(jax.random.fold_in(arg_keys[6], 71), 0),
        "first_kernel": bell_draw(arg_keys[1], (3, 3, 3, CHANNELS), 27 ** -0.5, 1.25),
        "second_kernel": bell_draw(arg_keys[2], (3, 3, 3, CHANNELS, CHANNELS), (27 * CHANNELS) ** -0.5, 0.21875),
        "class_weights": draw_class_weights(jax.random.fold_in(arg_keys[6], 71), 0),
        "patch_corners": draw_patch_corners(jax.random.fold_in(arg_keys[6], 71), 0),
        "patch_counts": draw_patch_counts(jax.random.fold_in(arg_keys[6], 71), 0),
    }


def untile(tile_block):
    cube_six = tile_block.reshape(2, 2, 2, HALF, HALF, HALF)
    return cube_six.transpose(0, 3, 1, 4, 2, 5).reshape(PATCH, PATCH, PATCH)

def retile(field_in):
    classes_here = field_in.shape[0]
    seven = field_in.reshape(classes_here, 2, HALF, 2, HALF, 2, HALF)
    return seven.transpose(1, 3, 5, 0, 2, 4, 6).reshape(2, 2, 2, classes_here, TILE_VOX)

def blend_map():
    coordinate = jnp.arange(PATCH, dtype=jnp.float32)
    center = (PATCH - 1) / 2.0
    spread = PATCH / 8.0
    square = (coordinate - center) ** 2 / (2.0 * spread * spread)
    total = square[:, None, None] + square[None, :, None] + square[None, None, :]
    return 0.1 + 0.9 * jnp.exp(-total)

def activate(field_in):
    channel_mean = lax.optimization_barrier(jnp.mean(field_in, axis=(1, 2, 3), keepdims=True))
    variance = lax.optimization_barrier(jnp.mean((field_in - channel_mean) ** 2, axis=(1, 2, 3), keepdims=True))
    normed = (field_in - channel_mean) * lax.rsqrt(variance + 1e-05)
    return jnp.where(normed > 0, normed, 0.01 * normed)

def correlate(field_in, kernel):
    return lax.conv_general_dilated(field_in[None], kernel, (1, 1, 1), 'SAME', dimension_numbers=('NCDHW', 'DHWIO', 'NCDHW'), precision=lax.Precision.HIGHEST)[0]

def network(cube, first_kernel, second_kernel, class_weights):
    inputs = cube.astype(jnp.float32)[None]
    first = correlate(inputs, first_kernel.astype(jnp.float32).reshape(3, 3, 3, 1, CHANNELS))
    hidden_one = activate(first).astype(jnp.bfloat16)
    second = correlate(hidden_one.astype(jnp.float32), second_kernel.astype(jnp.float32))
    hidden_two = activate(second)
    logits = jnp.einsum('ck,cxyz->kxyz', class_weights.astype(jnp.float32), hidden_two, precision=lax.Precision.HIGHEST)
    class_prob = jax.nn.softmax(logits, axis=0)
    return (blend_map()[None] * class_prob).astype(jnp.bfloat16)

def reference(volume, first_kernel, second_kernel, class_weights, patch_corners, patch_counts):
    class_sums = jnp.zeros((TILES_X, TILES_Y, TILES_Z, CLASSES, TILE_VOX), jnp.float32)
    weight_sums = jnp.zeros((TILES_X, TILES_Y, TILES_Z, TILE_VOX), jnp.float32)
    tiled_blend = retile(blend_map()[None])[:, :, :, 0]
    corner_list = patch_corners.reshape(TILES_X * HOME_MOST, 3).astype(jnp.int32)
    live_list = (jnp.arange(HOME_MOST)[None, :] < patch_counts[:, None]).reshape(-1)
    zero_index = jnp.zeros((), jnp.int32)

    def visit(running, entry_pair):
        sums_now, weights_now = running
        corner, live = entry_pair

        def work():
            tile_block = lax.dynamic_slice(volume, (corner[0], corner[1], corner[2], zero_index), (2, 2, 2, TILE_VOX))
            weighted = network(untile(tile_block), first_kernel, second_kernel, class_weights)
            return (retile(weighted).astype(jnp.float32), tiled_blend)

        def skip():
            return (jnp.zeros((2, 2, 2, CLASSES, TILE_VOX), jnp.float32), jnp.zeros((2, 2, 2, TILE_VOX), jnp.float32))
        added, blend_added = lax.cond(live, work, skip)
        start_five = (corner[0], corner[1], corner[2], zero_index, zero_index)
        old_sums = lax.dynamic_slice(sums_now, start_five, (2, 2, 2, CLASSES, TILE_VOX))
        sums_now = lax.dynamic_update_slice(sums_now, old_sums + added, start_five)
        start_four = (corner[0], corner[1], corner[2], zero_index)
        old_weights = lax.dynamic_slice(weights_now, start_four, (2, 2, 2, TILE_VOX))
        weights_now = lax.dynamic_update_slice(weights_now, old_weights + blend_added, start_four)
        return ((sums_now, weights_now), None)
    (class_sums, weight_sums), unused = lax.scan(visit, (class_sums, weight_sums), (corner_list, live_list))
    return class_sums / jnp.maximum(weight_sums, 0.1)[:, :, :, None, :]
```

```python
import jax
import jax.numpy as jnp
import numpy as np
from jax import lax
from jax.experimental import pallas as pl
from jax.experimental.pallas import tpu as pltpu
from jax.sharding import PartitionSpec as P

PATCH = 32
HALF = 16
TILE_VOX = 4096
CHANNELS = 32
CLASSES = 3
SENT = 2
HOME_MOST = 6
TILES_Y = 4
TILES_Z = 64
F32 = jnp.float32
BF16 = jnp.bfloat16
MIB = 1024 * 1024


def select_x():
    out = np.zeros((4, 16, 32), np.float32)
    for wx in range(4):
        for bx in range(16):
            x = 2 * bx - 1 + wx
            if 0 <= x < 32:
                out[wx, bx, x] = 1
    return out.reshape(64, 32)


def select_window():
    out = np.zeros((4, 2, 2, 16, 3, 4, 2, 16), np.float32)
    for wx in range(4):
        for ypar in range(2):
            for g in range(3):
                for zw in range(16):
                    z = 12 * g - 2 + zw
                    if 0 <= z < 32:
                        out[wx, z // 16, ypar, z % 16, g, wx, ypar, zw] = 1
    return out.reshape(256, 384)


def spread_first():
    out = np.zeros((6, 2, 4, 2, 16, 2, 2, 2, 32), np.float32)
    for j in range(6):
        for xpar in range(2):
            for sy in range(2):
                for sz in range(2):
                    for tap in range(27):
                        dx, dy, dz = tap // 9, tap // 3 % 3, tap % 3
                        wy = sy + dy
                        out[j, wy // 2, xpar + dx, wy % 2, 2 * j + sz + dz, xpar, sy, sz, tap] = 1
    return out.reshape(6 * 256, 256)


def blend_map():
    coordinate = np.arange(PATCH, dtype=np.float32)
    square = (coordinate - np.float32(15.5)) ** 2 / np.float32(32.0)
    total = square[:, None, None] + square[None, :, None] + square[None, None, :]
    return (np.float32(0.1) + np.float32(0.9) * np.exp(-total)).astype(np.float32)


def blend_rows():
    b = blend_map().reshape(16, 2, 16, 2, 2, 16)
    return b.transpose(2, 0, 4, 1, 3, 5).reshape(256, 128)


def blend_parts():
    b = blend_map().reshape(2, 16, 2, 16, 2, 16).transpose(0, 2, 4, 1, 3, 5).reshape(2, 4, TILE_VOX)
    out = np.zeros((4, 64, TILE_VOX), np.float32)
    for side in range(2):
        for patch in range(HOME_MOST):
            at = 24 * side + 4 * patch
            rest = b[side]
            for part in range(3):
                top = rest.astype(jnp.bfloat16).astype(np.float32)
                out[part, at : at + 4] = top
                rest = rest - top
    return out.reshape(256, TILE_VOX)


def call(kernel, vmem, **options):
    params = pltpu.CompilerParams(vmem_limit_bytes=vmem * MIB)
    return pl.pallas_call(kernel, compiler_params=params, **options)


SMEM_SPEC = pl.BlockSpec(memory_space=pltpu.SMEM)
VMEM_SPEC = pl.BlockSpec(memory_space=pltpu.VMEM)


def plan_kernel(column_ref, count_ref, plan_ref, sent):
    column = column_ref[0]

    def group_plan(group, at):
        counts = [count_ref[4 * group + i] for i in range(4)]
        heavy, seen = [], jnp.int32(0)
        for i in range(4):
            is_heavy = jnp.where((counts[i] == HOME_MOST) & (seen == 0), 1, 0)
            seen = seen + is_heavy
            heavy.append(is_heavy)
        room = [jnp.where(heavy[i] == 1, 0, jnp.maximum(2 - counts[i], 0)) for i in range(4)]
        extra = [jnp.where(heavy[i] == 1, 0, jnp.maximum(counts[i] - 2, 0)) for i in range(4)]
        for i in range(4):
            for j in range(4):
                if i == j:
                    continue
                give = jnp.where((extra[i] > 0) & (room[j] > 0), 1, 0)
                extra[i] = extra[i] - give
                room[j] = room[j] - give
                sent[at + 4 * i + j] = heavy[i] + give

    def column_plan(where, at, out):
        me = where % 4
        flags = [sent[at + 4 * me + (me + d) % 4] for d in (1, 2, 3)]
        kept = count_ref[where] - flags[0] - flags[1] - flags[2]
        slot = kept
        plan_ref[out] = kept
        for d in range(3):
            plan_ref[out + 1 + d] = flags[d]
            plan_ref[out + 4 + d] = jnp.minimum(slot, HOME_MOST - 1)
            slot = slot + flags[d]

    group_plan(column // 4, 0)
    column_plan(column, 0, 0)
    before = jnp.maximum(column - 1, 0)
    group_plan(before // 4, 16)
    column_plan(before, 16, 7)

    @pl.when(column == 0)
    def _():
        for i in range(4):
            plan_ref[7 + i] = 0

    me = column % 4
    plan_ref[15] = 0
    plan_ref[16] = 0
    plan_ref[17] = 0
    got = jnp.int32(0)
    for d in (1, 2, 3):
        flag = sent[4 * ((me + 4 - d) % 4) + me]

        @pl.when(flag == 1)
        def _():
            plan_ref[15 + got] = d - 1

        got = got + flag
    plan_ref[14] = got


def make_plan(column, patch_counts):
    return call(
        plan_kernel,
        2,
        out_shape=jax.ShapeDtypeStruct((18,), jnp.int32),
        in_specs=[SMEM_SPEC, SMEM_SPEC],
        out_specs=SMEM_SPEC,
        scratch_shapes=[pltpu.SMEM((32,), jnp.int32)],
        name="plan",
    )(column, patch_counts)


def gather_kernel(plan_ref, own_ref, prev_ref, volume_ref, own_out, prev_out, flat):
    for ty in range(TILES_Y):
        for group in range(TILES_Z // 16):
            for lane_tile in range(32):
                block = volume_ref[ty, 16 * group : 16 * group + 16, 128 * lane_tile : 128 * lane_tile + 128].astype(F32)
                for half in range(2):
                    start = ((ty * 8 + 2 * group + half) * 32 + lane_tile) * 8
                    flat[start : start + 8, :] = block[8 * half : 8 * half + 8]

    def take(corner_ref, out_ref, slot, place):
        for tile in range(4):
            ty = corner_ref[1, 0, slot] + tile // 2
            tz = corner_ref[2, 0, slot] + tile % 2
            base = (ty * 8 + tz // 8) * 256 + tz % 8
            rows = []
            for x_half in range(2):
                parts = [flat[pl.ds(base + 128 * x_half + 8 * h, 8, stride=16), :] for h in range(2)]
                rows.append(jnp.concatenate(parts, axis=1))
            out_ref[place, tile] = jnp.concatenate(rows, axis=0).astype(BF16)

    for at, corner_ref, out_ref in ((0, own_ref, own_out), (7, prev_ref, prev_out)):

        @pl.loop(0, plan_ref[at])
        def _(slot):
            take(corner_ref, out_ref, slot, slot)

        for d in range(3):

            @pl.when(plan_ref[at + 1 + d] == 1)
            def _():
                take(corner_ref, out_ref, plan_ref[at + 4 + d], 3 + d)


def gather(plan, corners, prev_corners, volume):
    shape = jax.ShapeDtypeStruct((HOME_MOST, 4, 16, 256), BF16)
    return call(
        gather_kernel,
        12,
        out_shape=(shape, shape),
        in_specs=[SMEM_SPEC, SMEM_SPEC, SMEM_SPEC, VMEM_SPEC],
        out_specs=(VMEM_SPEC, VMEM_SPEC),
        scratch_shapes=[pltpu.VMEM((TILES_Y * TILES_Z * 32, 128), F32)],
        name="gather_tiles",
    )(plan, corners, prev_corners, volume)


def dot(a, b):
    return jnp.dot(a, b, preferred_element_type=F32)


def weights_kernel(spread_ref, first_ref, second_ref, class_ref, first_out, second_out, class_out, four):
    lane = lax.broadcasted_iota(jnp.int32, (32, 256), 1)
    first = first_ref[...]
    blocks = [jnp.where(lane // 32 == s, first, 0.0).astype(BF16) for s in range(8)]
    big = jnp.concatenate(blocks, axis=0)
    for j in range(6):
        first_out[j] = dot(spread_ref[256 * j : 256 * j + 256, :], big).astype(BF16)

    part = lax.broadcasted_iota(jnp.int32, (32, 128), 1) // 32
    for tap in range(27):
        four[tap] = jnp.concatenate([second_ref[tap].astype(F32)] * 4, axis=1)
    for qx in range(4):
        for qy in range(4):
            for qz in range(4):
                at = ((((qy // 2 * 2 + qz // 2) * 2 + qx // 2) * 2 + qx % 2) * 2 + qy % 2) * 2 + qz % 2
                for half in range(2):
                    got = jnp.zeros((32, 128), F32)
                    for s in range(4):
                        dx, dy, dz = qx - half, qy - s // 2, qz - s % 2
                        if min(dx, dy, dz) >= 0 and max(dx, dy, dz) <= 2:
                            got = jnp.where(part == s, four[(dx * 3 + dy) * 3 + dz], got)
                    second_out[32 * at : 32 * at + 32, 128 * half : 128 * half + 128] = got.astype(BF16)

    columns = jnp.zeros((32, 256), F32)
    for k in range(CLASSES):
        columns = jnp.where(lane // 64 == k, class_ref[:, k : k + 1], columns)
    for b in range(8):
        for s in range(8):
            place = 32 * (s // 4) + 16 * (s // 2 % 2) + 2 * b + s % 2
            class_out[b, 32 * s : 32 * s + 32, :] = jnp.where(lane % 64 == place, columns, 0.0).astype(BF16)


def raw_weights(first_kernel, second_kernel, class_weights):
    first = jnp.pad(first_kernel.reshape(27, CHANNELS), ((0, 5), (0, 0))).astype(F32)
    return (
        jnp.tile(first, (1, 8)),
        second_kernel.reshape(27, CHANNELS, CHANNELS),
        jnp.pad(class_weights.astype(F32), ((0, 0), (0, 128 - CLASSES))),
    )


def prepare_weights(first, second, classes):
    return call(
        weights_kernel,
        12,
        out_shape=(
            jax.ShapeDtypeStruct((6, 256, 256), BF16),
            jax.ShapeDtypeStruct((2048, 256), BF16),
            jax.ShapeDtypeStruct((8, 256, 256), BF16),
        ),
        in_specs=[VMEM_SPEC] * 4,
        out_specs=(VMEM_SPEC,) * 3,
        scratch_shapes=[pltpu.VMEM((27, 32, 128), F32)],
        cost_estimate=pl.CostEstimate(flops=1_000_000_000, bytes_accessed=8_000_000, transcendentals=0),
        name="weights",
    )(jnp.asarray(spread_first(), BF16), first, second, classes)


def fold_channels(row):
    half = row[:, :128] + row[:, 128:]
    half = half + pltpu.roll(half, 64, 1)
    half = half + pltpu.roll(half, 32, 1)
    return jnp.concatenate([half, half], axis=1)


def merge_stats(pivot, s1, s2):
    count = 4096.0
    lane_mean = pivot + s1 * (1.0 / count)
    lane_m2 = s2 - s1 * s1 * (1.0 / count)
    mean = fold_channels(lane_mean) * 0.125
    off = lane_mean - mean
    var = fold_channels(lane_m2 + count * (off * off)) * (1.0 / 32768.0)
    return mean, lax.rsqrt(var + 1e-05)


def leaky(v):
    return jnp.maximum(v, 0.01 * v)


def sum_rows(block):
    return jnp.sum(block, axis=0, keepdims=True)


def network_kernel(plan_ref, low_ref, up_ref, *refs):
    sent_refs, refs = refs[:3], refs[3:]
    pick_ref, window_ref, first_ref, second_ref, class_ref, blend_ref = refs[:6]
    outs, (cubes, made, spread, raw, hidden, second, logits) = refs[6:-7], refs[-7:]
    for i in range(3):
        cubes[i, 0] = low_ref[i]
        cubes[i, 1] = up_ref[i]
        cubes[3 + i] = sent_refs[i][...]

    spread[0] = jnp.zeros((16, 384), BF16)
    spread[17] = jnp.zeros((16, 384), BF16)
    lane = lax.broadcasted_iota(jnp.int32, (1, 256), 1)
    sy, sz = (lane % 128) // 64, (lane % 64) // 32
    y_first = (sy == 1).astype(F32)
    y_last = (sy == 0).astype(F32)
    row16 = lax.broadcasted_iota(jnp.int32, (16, 128), 0)
    lane16 = lax.broadcasted_iota(jnp.int32, (16, 128), 1) // 32

    def z_mask(bz):
        bad = ((bz == 0) & (sz == 0)) | ((bz == 16) & (sz == 1))
        return jnp.where(bad, 0.0, 1.0)

    def patch(index, carry):
        kept = plan_ref[0]
        slot = jnp.where(index < kept, index, 3 + plan_ref[15 + jnp.maximum(index - kept, 0)])
        cube = jnp.concatenate(
            [jnp.concatenate([cubes[slot, tx, t] for t in range(4)], axis=1) for tx in range(2)], axis=0
        )
        moved = dot(pick_ref[...], cube)
        lists = []
        for ty in range(2):
            for quad in range(2):
                pieces = []
                for wx in range(4):
                    for tz in range(2):
                        at = (ty * 2 + tz) * 256 + quad * 128
                        pieces.append(moved[16 * wx : 16 * wx + 16, at : at + 128])
                for r in range(4):
                    joined = []
                    for tile in range(2):
                        got = None
                        for place in range(4):
                            piece = pieces[4 * tile + place]
                            turn = (32 * (place - r)) % 128
                            if turn:
                                piece = pltpu.roll(piece, turn, 1)
                            got = piece if got is None else jnp.where(lane16 == place, piece, got)
                        joined.append(got)
                    lists.append(jnp.concatenate(joined, axis=1).astype(BF16))
        rows = jnp.concatenate(lists, axis=0)
        spread[1:17] = dot(rows, window_ref[...]).astype(BF16).reshape(16, 16, 384)

        for g in range(3):
            lanes = slice(128 * g, 128 * g + 128)
            lhs = jnp.concatenate([spread[0:17, :, lanes], spread[1:18, :, lanes]], axis=2).reshape(272, 256)
            for j in range(6):
                if 6 * g + j <= 16:
                    raw[6 * g + j] = dot(lhs, first_ref[j])

        pivot = sum_rows(raw[1, 16:256]) * (1.0 / 240.0)

        def plane_sums(bz):
            d = raw[bz] - pivot
            inner = d[16:256].reshape(15, 16, 256)
            edges = d[0:16] * y_first, d[256:272] * y_last
            s1 = jnp.sum(inner, axis=0) + (edges[0] + edges[1])
            s2 = jnp.sum(inner * inner, axis=0) + (edges[0] * edges[0] + edges[1] * edges[1])
            return s1, s2

        def gather_stats(bz, sums):
            a1, a2 = plane_sums(bz)
            return (sums[0] + a1, sums[1] + a2)

        first_plane, last_plane = plane_sums(0), plane_sums(16)
        start = [first_plane[i] * z_mask(0) + last_plane[i] * z_mask(16) for i in range(2)]
        s1, s2 = lax.fori_loop(1, 16, gather_stats, tuple(start))
        mean, inv = merge_stats(pivot, sum_rows(s1), sum_rows(s2))

        def normalise(bz, carry):
            scale = inv * z_mask(bz)
            for by in range(17):
                here = scale * y_first if by == 0 else scale * y_last if by == 16 else scale
                v = leaky((raw[bz, 16 * by : 16 * by + 16] - mean) * here)
                even, odd = v[:, :128], v[:, 128:]
                before = jnp.where(row16 == 0, 0.0, pltpu.roll(odd, 1, 0))
                after = jnp.where(row16 == 15, 0.0, pltpu.roll(even, 15, 0))
                hidden[bz, by] = jnp.concatenate([before, even, odd, after], axis=1).astype(BF16)
            return carry

        lax.fori_loop(0, 17, normalise, 0)

        def second_slabs(pair):
            sides = []
            for i in range(2):
                bz = 2 * pair + i
                parts = [hidden[bz + ez, ey : ey + 16].reshape(256, 512) for ey in range(2) for ez in range(2)]
                sides.append(jnp.concatenate(parts, axis=1))
            slabs = dot(jnp.concatenate(sides, axis=0), second_ref[...])
            second[pl.ds(2 * pair, 2)] = slabs.reshape(2, 256, 256)
            return slabs

        def slab_sums(slabs, pivot):
            d = (slabs - pivot).reshape(32, 16, 256)
            return jnp.sum(d, axis=0), jnp.sum(d * d, axis=0)

        slabs = second_slabs(0)
        pivot2 = sum_rows(slabs) * (1.0 / 512.0)

        def second_loop(pair, sums):
            a1, a2 = slab_sums(second_slabs(pair), pivot2)
            return (sums[0] + a1, sums[1] + a2)

        s1, s2 = lax.fori_loop(1, 8, second_loop, slab_sums(slabs, pivot2))
        mean, inv = merge_stats(pivot2, sum_rows(s1), sum_rows(s2))

        for tz in range(2):
            acc = None
            for b in range(8):
                h = leaky((second[8 * tz + b] - mean) * inv)
                top = h.astype(BF16)
                rest = (h - top.astype(F32)).astype(BF16)
                weights = class_ref[b]
                add = dot(top, weights) + dot(rest, weights)
                acc = add if acc is None else acc + add
            logits[tz] = acc

        side = lax.broadcasted_iota(jnp.int32, (256, 128), 1) < 64
        t0, t1 = logits[0, :, 0:128], logits[0, :, 128:256]
        u0, u1 = logits[1, :, 0:128], logits[1, :, 128:256]
        l0 = jnp.where(side, t0, pltpu.roll(u0, 64, 1))
        l1 = jnp.where(side, pltpu.roll(t0, 64, 1), u0)
        l2 = jnp.where(side, t1, pltpu.roll(u1, 64, 1))
        most = jnp.maximum(jnp.maximum(l0, l1), l2)
        x0, x1, x2 = jnp.exp(l0 - most), jnp.exp(l1 - most), jnp.exp(l2 - most)
        share = blend_ref[...] / (x0 + x1 + x2)

        lane32 = lax.broadcasted_iota(jnp.int32, (64, 128), 1) // 32
        for k, x in enumerate((x0, x1)):
            w = (x * share).reshape(4, 4, 16, 128)
            sources = [w[:, r].reshape(64, 128) for r in range(4)]
            dest = []
            for q in range(4):
                got = None
                for r in range(4):
                    turn = (32 * (r - q)) % 128
                    piece = pltpu.roll(sources[r], turn, 1) if turn else sources[r]
                    got = piece if got is None else jnp.where(lane32 == r, piece, got)
                dest.append(got)
            for tx in range(2):
                for ty in range(2):
                    for h in range(2):
                        at = (2 * ty + h) * 16 + 8 * tx
                        for tz in range(2):
                            both = jnp.concatenate([dest[2 * tz][at : at + 8], dest[2 * tz + 1][at : at + 8]], axis=0)
                            rows = slice(16 * k, 16 * k + 16)
                            lanes = slice(128 * h, 128 * h + 128)
                            made[tx, slot, 2 * ty + tz, rows, lanes] = both.astype(BF16)
        return carry

    lax.fori_loop(0, plan_ref[0] + plan_ref[14], patch, 0)
    outs[0][...] = made[0, 0:3]
    outs[1][...] = made[1, 0:3]
    for d in range(3):
        outs[2 + d][...] = made[0, 3 + d]
        outs[5 + d][...] = made[1, 3 + d]


def network(plan, low, up, sent, weights):
    one = jax.ShapeDtypeStruct((4, 16 * SENT, 256), BF16)
    three = jax.ShapeDtypeStruct((3, 4, 16 * SENT, 256), BF16)
    outs = call(
        network_kernel,
        32,
        out_shape=(three,) * 2 + (one,) * 6,
        in_specs=[SMEM_SPEC] + [VMEM_SPEC] * 11,
        out_specs=(VMEM_SPEC,) * 8,
        scratch_shapes=[
            pltpu.VMEM((6, 2, 4, 16, 256), BF16),
            pltpu.VMEM((2, 6, 4, 16 * SENT, 256), BF16),
            pltpu.VMEM((18, 16, 384), BF16),
            pltpu.VMEM((17, 272, 256), F32),
            pltpu.VMEM((17, 17, 16, 512), BF16),
            pltpu.VMEM((16, 256, 256), F32),
            pltpu.VMEM((2, 256, 256), F32),
        ],
        cost_estimate=pl.CostEstimate(flops=20_000_000_000, bytes_accessed=8_000_000, transcendentals=600_000),
        name="network",
    )(plan, low, up, *sent, *weights)
    return outs[0], outs[1], outs[2:5], outs[5:8]


def patch_entry(plan_ref, side, i):
    at = 7 * side
    if i < 3:
        return i < plan_ref[at], i
    return plan_ref[at + i - 2] == 1, plan_ref[at + i + 1]


def inverse_kernel(plan_ref, own_ref, prev_ref, parts_ref, inverse_ref, chosen_ref, chosen_parts):
    @pl.when(pl.program_id(0) == 0)
    def _():
        lane = lax.broadcasted_iota(jnp.int32, (1, 256), 1) % 64
        tiles = jnp.full((1, 256), -1, jnp.int32)
        for side, corner_ref in enumerate((own_ref, prev_ref)):
            for i in range(HOME_MOST):
                live, slot = patch_entry(plan_ref, side, i)
                first = corner_ref[1, 0, slot] * TILES_Z + corner_ref[2, 0, slot]
                for t in range(4):
                    tile = jnp.where(live, first + TILES_Z * (t // 2) + t % 2, -1)
                    tiles = jnp.where(lane == 24 * side + 4 * i + t, tile, tiles)
        same = lax.broadcasted_iota(jnp.int32, (256, 256), 0) == tiles
        hot = jnp.where(same, 1.0, 0.0).astype(BF16)
        chosen_parts[...] = hot
        chosen_ref[...] = hot[:, :128]

    weight = dot(chosen_parts[...], parts_ref[...])
    inverse_ref[...] = jnp.where(weight > 0, 1.0 / jnp.maximum(weight, 0.1), 0.0)


def inverse_weights(plan, corners, prev_corners):
    return call(
        inverse_kernel,
        12,
        grid=(4,),
        out_shape=(
            jax.ShapeDtypeStruct((TILES_Y * TILES_Z, TILE_VOX), F32),
            jax.ShapeDtypeStruct((TILES_Y * TILES_Z, 128), BF16),
        ),
        in_specs=[SMEM_SPEC] * 3 + [pl.BlockSpec((256, 1024), lambda i: (0, i))],
        out_specs=(pl.BlockSpec((256, 1024), lambda i: (0, i)), pl.BlockSpec((256, 128), lambda i: (0, 0))),
        scratch_shapes=[pltpu.VMEM((256, 256), BF16)],
        cost_estimate=pl.CostEstimate(flops=1_000_000_000, bytes_accessed=8_000_000, transcendentals=0),
        name="inverse_weights",
    )(plan, corners, prev_corners, jnp.asarray(blend_parts(), BF16))


def blend_kernel(plan_ref, chosen_ref, inverse_ref, low_ref, *refs):
    sides = ((low_ref, refs[0:3]), (refs[3], refs[4:7]))
    out_ref, rows, stacked = refs[7:]
    step = pl.program_id(0)

    @pl.when(step == 0)
    def _():
        for side, (kept_ref, sent_refs) in enumerate(sides):
            for i in range(HOME_MOST):
                live, _ = patch_entry(plan_ref, side, i)

                @pl.when(live)
                def _():
                    for t in range(4):
                        at = 40 * (24 * side + 4 * i + t)
                        for h in range(2):
                            lanes = slice(128 * h, 128 * h + 128)
                            part = kept_ref[i, t, :, lanes] if i < 3 else sent_refs[i - 3][t, :, lanes]
                            rows[h, at : at + 16 * SENT, :] = part.astype(F32)

                @pl.when(jnp.logical_not(live))
                def _():
                    at = 40 * (24 * side + 4 * i)
                    for h in range(2):
                        rows[h, at : at + 160, :] = jnp.zeros((160, 128), F32)

        for x in range(16):
            stacked[x, 48:64, :] = jnp.zeros((16, 256 * SENT), BF16)
            for k in range(SENT):
                row = 16 * k + (x % 2) * 8 + x // 2
                for h in range(2):
                    for pair in range(3):
                        both = [rows[h, pl.ds(640 * pair + 320 * o + row, 8, stride=40), :] for o in range(2)]
                        at = 256 * k + 128 * h
                        stacked[x, 16 * pair : 16 * pair + 16, at : at + 128] = jnp.concatenate(both, axis=0).astype(BF16)

    for x in range(2):
        lanes = slice(256 * x, 256 * x + 256)
        inv = inverse_ref[:, lanes]
        got = dot(chosen_ref[:, 0:64], stacked[2 * step + x])
        p0, p1 = got[:, :256] * inv, got[:, 256:] * inv
        p2 = jnp.where(inv > 0, jnp.maximum(1.0 - p0 - p1, 0.0), 0.0)
        for k, p in enumerate((p0, p1, p2)):
            out_ref[:, k, :, lanes] = p.reshape(TILES_Y, TILES_Z, 256)


def blend(plan, chosen, inverse, low, low_sent, ghost, ghost_sent):
    return call(
        blend_kernel,
        16,
        grid=(8,),
        out_shape=jax.ShapeDtypeStruct((TILES_Y, CLASSES, TILES_Z, TILE_VOX), F32),
        in_specs=[SMEM_SPEC, VMEM_SPEC, pl.BlockSpec((256, 512), lambda i: (0, i))] + [VMEM_SPEC] * 8,
        out_specs=pl.BlockSpec((TILES_Y, CLASSES, TILES_Z, 512), lambda i: (0, 0, 0, i)),
        scratch_shapes=[
            pltpu.VMEM((2, 48 * 40, 128), F32),
            pltpu.VMEM((16, 64, 256 * SENT), BF16),
        ],
        name="blend",
    )(plan, chosen, inverse, low, *low_sent, ghost, *ghost_sent)


def passed_along(block, axis, distance):
    devices = range(lax.axis_size(axis))
    route = [(i - distance, i) for i in devices if i - distance in devices]
    return lax.ppermute(block, axis, route)


def passed_round(block, distance):
    size = lax.axis_size("bal")
    return lax.ppermute(block, "bal", [(i, (i + distance) % size) for i in range(size)])


def passed_after_home(block, distance):
    axes = ("slab", "bal")
    route = []
    for i in range(lax.axis_size(axes)):
        home = i // 4 * 4 + (i - distance) % 4
        if home + 1 < lax.axis_size(axes):
            route.append((i, home + 1))
    return lax.ppermute(block, axes, route)


def local(volume, first_kernel, second_kernel, class_weights, patch_corners, patch_counts):
    axes = ("slab", "bal")
    column = lax.axis_index(axes).astype(jnp.int32)
    corners = patch_corners.transpose(2, 0, 1)
    prev_corners = passed_along(corners, axes, 1)
    plan = make_plan(column[None], patch_counts)
    own_tiles, prev_tiles = gather(plan, corners, prev_corners, volume[0])
    next_tiles = passed_along(prev_tiles, axes, -1)
    raw = raw_weights(first_kernel, second_kernel, class_weights)
    raw, corners, prev_corners, own_tiles = lax.optimization_barrier((raw, corners, prev_corners, own_tiles))
    inverse, chosen = inverse_weights(plan, corners, prev_corners)
    inverse, chosen, next_tiles = lax.optimization_barrier((inverse, chosen, next_tiles))
    weights = (
        jnp.asarray(select_x(), BF16),
        jnp.asarray(select_window(), BF16),
        *prepare_weights(*raw),
        jnp.asarray(blend_rows(), F32),
    )
    shipped = [
        passed_round(jnp.concatenate([own_tiles[2 + d : 3 + d], next_tiles[2 + d : 3 + d]], axis=0), d) for d in (1, 2, 3)
    ]
    low, up, low_done, up_done = network(plan, own_tiles, next_tiles, shipped, weights)
    ghost = passed_along(up, axes, 1)
    low_sent = [passed_round(low_done[d - 1], -d) for d in (1, 2, 3)]
    ghost_sent = [passed_after_home(up_done[d - 1], d) for d in (1, 2, 3)]
    out = blend(plan, chosen, inverse, low, low_sent, ghost, ghost_sent)
    return out.transpose(0, 2, 1, 3)[None]


def solution(mesh):
    return jax.shard_map(
        local,
        mesh=mesh,
        in_specs=(
            P(("slab", "bal"), None, None, None),
            P(),
            P(),
            P(),
            P(("slab", "bal"), None, None),
            P(),
        ),
        out_specs=P(("slab", "bal"), None, None, None, None),
        check_vma=False,
    )
```

```python
import jax
import jax.numpy as jnp
import numpy as np
from jax import lax
from jax.experimental import pallas as pl
from jax.experimental.pallas import tpu as pltpu
from jax.sharding import PartitionSpec as P

PATCH = 32
HALF = 16
TILE_VOX = 4096
CHANNELS = 32
CLASSES = 3
ENTRIES = 7
SENT = 2
HOME_MOST = 6
TILES_Y = 4
TILES_Z = 64
F32 = jnp.float32
BF16 = jnp.bfloat16
MIB = 1024 * 1024


def select_x():
    out = np.zeros((4, 16, 32), np.float32)
    for wx in range(4):
        for bx in range(16):
            x = 2 * bx - 1 + wx
            if 0 <= x < 32:
                out[wx, bx, x] = 1
    return out.reshape(64, 32)


def select_window():
    out = np.zeros((4, 2, 2, 16, 3, 4, 2, 16), np.float32)
    for wx in range(4):
        for ypar in range(2):
            for g in range(3):
                for zw in range(16):
                    z = 12 * g - 2 + zw
                    if 0 <= z < 32:
                        out[wx, z // 16, ypar, z % 16, g, wx, ypar, zw] = 1
    return out.reshape(256, 384)


def blend_map():
    coordinate = np.arange(PATCH, dtype=np.float32)
    square = (coordinate - np.float32(15.5)) ** 2 / np.float32(32.0)
    total = square[:, None, None] + square[None, :, None] + square[None, None, :]
    return (np.float32(0.1) + np.float32(0.9) * np.exp(-total)).astype(np.float32)


def blend_rows():
    b = blend_map().reshape(16, 2, 16, 2, 2, 16)
    return b.transpose(2, 0, 4, 1, 3, 5).reshape(256, 128)


def blend_parts():
    b = blend_map().reshape(2, 16, 2, 16, 2, 16).transpose(0, 2, 4, 1, 3, 5).reshape(2, 4, TILE_VOX)
    out = np.zeros((4, 64, TILE_VOX), np.float32)
    for side in range(2):
        for patch in range(ENTRIES):
            at = 4 * (ENTRIES * side + patch)
            rest = b[side]
            for part in range(3):
                top = rest.astype(jnp.bfloat16).astype(np.float32)
                out[part, at : at + 4] = top
                rest = rest - top
    return out.reshape(256, TILE_VOX)


def call(kernel, vmem, **options):
    params = pltpu.CompilerParams(vmem_limit_bytes=vmem * MIB)
    return pl.pallas_call(kernel, compiler_params=params, **options)


SMEM_SPEC = pl.BlockSpec(memory_space=pltpu.SMEM)
VMEM_SPEC = pl.BlockSpec(memory_space=pltpu.VMEM)


def plan_kernel(column_ref, count_ref, plan_ref, sent):
    column = column_ref[0]

    def group_plan(group, at):
        heavy = jnp.int32(0)
        for i in (3, 2, 1, 0):
            heavy = jnp.where(count_ref[4 * group + i] == HOME_MOST, i, heavy)
        place = [(heavy + k) % 4 for k in range(4)]
        count = [count_ref[4 * group + place[k]] for k in range(4)]
        left = [jnp.where((count[1] >= 4) & (heavy >= 1), 1, 0), 0, 0, 0]
        right = []
        coming = 0
        for k in range(4):
            load = count[k] + coming - left[k]
            if k == 3:
                load = load + left[0]
                left[3] = jnp.where((load > 3) & (place[3] >= 1), 1, 0)
                load = load - left[3]
            out = jnp.clip(load - 3, 0, jnp.minimum(count[k] - left[k], 3))
            right.append(out)
            coming = out
        for k in range(4):
            sent[at + place[k]] = right[k]
            sent[at + 4 + place[k]] = left[k]

    def column_plan(where, at, out):
        me = where % 4
        right, left = sent[at + me], sent[at + 4 + me]
        plan_ref[out] = count_ref[where] - right - left
        plan_ref[out + 1] = right
        plan_ref[out + 2] = left

    group_plan(column // 4, 0)
    column_plan(column, 0, 0)
    me = column % 4
    plan_ref[6] = sent[(me + 3) % 4]
    plan_ref[7] = jnp.where(me == 3, 0, sent[4 + (me + 1) % 4])
    plan_ref[8] = jnp.where(me == 0, 1, 0)
    before = jnp.maximum(column - 1, 0)
    group_plan(before // 4, 8)
    column_plan(before, 8, 3)

    @pl.when(column == 0)
    def _():
        for i in range(3):
            plan_ref[3 + i] = 0


def make_plan(column, patch_counts):
    return call(
        plan_kernel,
        2,
        out_shape=jax.ShapeDtypeStruct((9,), jnp.int32),
        in_specs=[SMEM_SPEC, SMEM_SPEC],
        out_specs=SMEM_SPEC,
        scratch_shapes=[pltpu.SMEM((16,), jnp.int32)],
        name="plan",
    )(column, patch_counts)


def flatten_kernel(volume_ref, flat, staged, arrived):
    copies = [pltpu.make_async_copy(volume_ref.at[ty], staged.at[ty], arrived.at[ty]) for ty in range(TILES_Y)]
    for copy in copies:
        copy.start()
    for ty in range(TILES_Y):
        copies[ty].wait()
        for group in range(TILES_Z // 16):
            for lane_tile in range(32):
                block = staged[ty, 16 * group : 16 * group + 16, 128 * lane_tile : 128 * lane_tile + 128].astype(F32)
                for half in range(2):
                    start = ((ty * 8 + 2 * group + half) * 32 + lane_tile) * 8
                    flat[start : start + 8, :] = block[8 * half : 8 * half + 8]


def flatten(volume):
    return call(
        flatten_kernel,
        12,
        out_shape=jax.ShapeDtypeStruct((TILES_Y * TILES_Z * 32, 128), F32),
        in_specs=[pl.BlockSpec(memory_space=pl.ANY)],
        out_specs=VMEM_SPEC,
        scratch_shapes=[pltpu.VMEM((TILES_Y, TILES_Z, TILE_VOX), BF16), pltpu.SemaphoreType.DMA((TILES_Y,))],
        cost_estimate=pl.CostEstimate(flops=2_000_000, bytes_accessed=6_000_000, transcendentals=0),
        name="flatten",
    )(volume)


def take_tiles(corner_ref, flat, out_ref, slot, place):
    for tile in range(4):
        ty = corner_ref[1, 0, slot] + tile // 2
        tz = corner_ref[2, 0, slot] + tile % 2
        base = (ty * 8 + tz // 8) * 256 + tz % 8
        rows = []
        for x_half in range(2):
            parts = [flat[pl.ds(base + 128 * x_half + 8 * h, 8, stride=16), :] for h in range(2)]
            rows.append(jnp.concatenate(parts, axis=1))
        out_ref[place, tile] = jnp.concatenate(rows, axis=0).astype(BF16)


def take_entries(plan_ref, at, corner_ref, flat, kept_out, right_out, left_out):
    kept, right = plan_ref[at], plan_ref[at + 1]

    @pl.loop(0, kept)
    def _(slot):
        take_tiles(corner_ref, flat, kept_out, slot, slot)

    @pl.loop(0, right)
    def _(slot):
        take_tiles(corner_ref, flat, right_out, kept + slot, slot)

    @pl.when(plan_ref[at + 2] == 1)
    def _():
        take_tiles(corner_ref, flat, left_out, kept + right, 0)


def gather_own_kernel(plan_ref, corner_ref, flat, kept_out, right_out, left_out):
    take_entries(plan_ref, 0, corner_ref, flat, kept_out, right_out, left_out)


def gather_next_kernel(plan_ref, corner_ref, flat, own_left, back_out, right_out, left_out):
    take_entries(plan_ref, 3, corner_ref, flat, back_out, right_out, left_out)
    back_out[3] = own_left[0]


def tiles(count):
    return jax.ShapeDtypeStruct((count, 4, 16, 256), BF16)


def gather_own(plan, corners, flat):
    return call(
        gather_own_kernel,
        8,
        out_shape=(tiles(3), tiles(3), tiles(1)),
        in_specs=[SMEM_SPEC, SMEM_SPEC, VMEM_SPEC],
        out_specs=(VMEM_SPEC,) * 3,
        name="gather_own",
    )(plan, corners, flat)


def gather_next(plan, prev_corners, flat, own_left):
    return call(
        gather_next_kernel,
        8,
        out_shape=(tiles(4), tiles(3), tiles(1)),
        in_specs=[SMEM_SPEC, SMEM_SPEC, VMEM_SPEC, VMEM_SPEC],
        out_specs=(VMEM_SPEC,) * 3,
        name="gather_next",
    )(plan, prev_corners, flat, own_left)


def dot(a, b):
    return jnp.dot(a, b, preferred_element_type=F32)


def weights_kernel(first_ref, second_ref, class_ref, first_out, second_out, class_out, four, taps, turned):
    lane = lax.broadcasted_iota(jnp.int32, (32, 256), 1)
    taps[...] = jnp.zeros((32, 32), F32)
    for dx in range(3):
        for dy in range(3):
            at = 9 * dx + 3 * dy
            taps[at : at + 3, :] = first_ref[dx, dy].astype(F32)
    first = jnp.concatenate([taps[...]] * 8, axis=1)
    big = jnp.concatenate([jnp.where(lane // 32 == s, first, 0.0).astype(BF16) for s in range(8)], axis=0)
    row = lax.broadcasted_iota(jnp.int32, (256, 256), 0)
    col = lax.broadcasted_iota(jnp.int32, (256, 256), 1)
    tap = col % 32
    dx = jnp.where(tap >= 18, 2, jnp.where(tap >= 9, 1, 0))
    rest = tap - 9 * dx
    dy = jnp.where(rest >= 6, 2, jnp.where(rest >= 3, 1, 0))
    dz = rest - 3 * dy
    fits = ((row // 32) % 4 == col // 128 + dx) & (row // 128 * 2 + (row // 16) % 2 == (col // 64) % 2 + dy) & (tap < 27)
    ahead = row % 16 - (col // 32) % 2 - dz
    for j in range(6):
        spread = jnp.where(fits & (ahead == 2 * j), 1.0, 0.0).astype(BF16)
        first_out[j] = dot(spread, big).astype(BF16)

    part = lax.broadcasted_iota(jnp.int32, (32, 128), 1) // 32
    for tap in range(27):
        four[tap] = jnp.concatenate([second_ref[tap].astype(F32)] * 4, axis=1)
    for qx in range(4):
        for qy in range(4):
            for qz in range(4):
                at = ((((qy // 2 * 2 + qz // 2) * 2 + qx // 2) * 2 + qx % 2) * 2 + qy % 2) * 2 + qz % 2
                for half in range(2):
                    got = jnp.zeros((32, 128), F32)
                    for s in range(4):
                        dx, dy, dz = qx - half, qy - s // 2, qz - s % 2
                        if min(dx, dy, dz) >= 0 and max(dx, dy, dz) <= 2:
                            got = jnp.where(part == s, four[(dx * 3 + dy) * 3 + dz], got)
                    second_out[32 * at : 32 * at + 32, 128 * half : 128 * half + 128] = got.astype(BF16)

    turned[...] = jnp.zeros((128, 128), F32)
    turned[0:CLASSES, 0:CHANNELS] = class_ref[...].astype(F32)
    classes = turned[...].T
    columns = jnp.zeros((32, 256), F32)
    for k in range(CLASSES):
        columns = jnp.where(lane // 64 == k, classes[0:32, k : k + 1], columns)
    for b in range(8):
        for s in range(8):
            place = 32 * (s // 4) + 16 * (s // 2 % 2) + 2 * b + s % 2
            class_out[b, 32 * s : 32 * s + 32, :] = jnp.where(lane % 64 == place, columns, 0.0).astype(BF16)


def prepare_weights(first_kernel, second_kernel, class_weights):
    return call(
        weights_kernel,
        12,
        out_shape=(
            jax.ShapeDtypeStruct((6, 256, 256), BF16),
            jax.ShapeDtypeStruct((2048, 256), BF16),
            jax.ShapeDtypeStruct((8, 256, 256), BF16),
        ),
        in_specs=[VMEM_SPEC] * 3,
        out_specs=(VMEM_SPEC,) * 3,
        scratch_shapes=[pltpu.VMEM((27, 32, 128), F32), pltpu.VMEM((32, 32), F32), pltpu.VMEM((128, 128), F32)],
        cost_estimate=pl.CostEstimate(flops=1_000_000_000, bytes_accessed=8_000_000, transcendentals=0),
        name="weights",
    )(first_kernel, second_kernel.reshape(27, CHANNELS, CHANNELS), class_weights.T)


def fold_channels(row):
    half = row[:, :128] + row[:, 128:]
    half = half + pltpu.roll(half, 64, 1)
    half = half + pltpu.roll(half, 32, 1)
    return jnp.concatenate([half, half], axis=1)


def merge_stats(pivot, s1, s2):
    count = 4096.0
    lane_mean = pivot + s1 * (1.0 / count)
    lane_m2 = s2 - s1 * s1 * (1.0 / count)
    mean = fold_channels(lane_mean) * 0.125
    off = lane_mean - mean
    var = fold_channels(lane_m2 + count * (off * off)) * (1.0 / 32768.0)
    return mean, lax.rsqrt(var + 1e-05)


def leaky(v):
    return jnp.maximum(v, 0.01 * v)


def sum_rows(block):
    return jnp.sum(block, axis=0, keepdims=True)


def network_kernel(plan_ref, own_ref, back_ref, right_ref, here_ref, across_ref, left_ref, *refs):
    pick_ref, window_ref, first_ref, second_ref, class_ref, blend_ref = refs[:6]
    outs, (cubes, made, spread, raw, hidden_a, hidden_b, second) = refs[6:-7], refs[-7:]
    for i in range(3):
        cubes[i, 0] = own_ref[i]
        cubes[i, 1] = back_ref[i]
        cubes[3 + i, 0] = right_ref[i]
    cubes[6, 0] = back_ref[3]
    cubes[6, 1] = left_ref[0]

    @pl.when(plan_ref[8] == 0)
    def _():
        for i in range(3):
            cubes[3 + i, 1] = here_ref[i]

    @pl.when(plan_ref[8] == 1)
    def _():
        for i in range(3):
            cubes[3 + i, 1] = across_ref[i]

    spread[0] = jnp.zeros((16, 384), BF16)
    spread[17] = jnp.zeros((16, 384), BF16)
    lane = lax.broadcasted_iota(jnp.int32, (1, 256), 1)
    sy, sz = (lane % 128) // 64, (lane % 64) // 32
    y_first = (sy == 1).astype(F32)
    y_last = (sy == 0).astype(F32)
    row16 = lax.broadcasted_iota(jnp.int32, (16, 128), 0)
    lane16 = lax.broadcasted_iota(jnp.int32, (16, 128), 1) // 32

    def z_mask(bz):
        bad = ((bz == 0) & (sz == 0)) | ((bz == 16) & (sz == 1))
        return jnp.where(bad, 0.0, 1.0)

    def patch(index, carry):
        kept = plan_ref[0]
        later = jnp.where(index - kept < plan_ref[6], 3 + index - kept, 6)
        slot = jnp.where(index < kept, index, later)
        cube = jnp.concatenate(
            [jnp.concatenate([cubes[slot, tx, t] for t in range(4)], axis=1) for tx in range(2)], axis=0
        )
        moved = dot(pick_ref[...], cube)
        lists = []
        for ty in range(2):
            for quad in range(2):
                pieces = []
                for wx in range(4):
                    for tz in range(2):
                        at = (ty * 2 + tz) * 256 + quad * 128
                        pieces.append(moved[16 * wx : 16 * wx + 16, at : at + 128])
                for r in range(4):
                    joined = []
                    for tile in range(2):
                        got = None
                        for place in range(4):
                            piece = pieces[4 * tile + place]
                            turn = (32 * (place - r)) % 128
                            if turn:
                                piece = pltpu.roll(piece, turn, 1)
                            got = piece if got is None else jnp.where(lane16 == place, piece, got)
                        joined.append(got)
                    lists.append(jnp.concatenate(joined, axis=1).astype(BF16))
        rows = jnp.concatenate(lists, axis=0)
        spread[1:17] = dot(rows, window_ref[...]).astype(BF16).reshape(16, 16, 384)

        def first_plane(bz):
            lanes = slice(128 * (bz // 6), 128 * (bz // 6) + 128)
            lhs = jnp.concatenate([spread[0:17, :, lanes], spread[1:18, :, lanes]], axis=2).reshape(272, 256)
            out = dot(lhs, first_ref[bz % 6])
            raw[bz] = out
            return out

        def plane_sums(bz, out, pivot):
            d = out - pivot
            inner = d[16:256].reshape(15, 16, 256)
            edges = d[0:16] * y_first, d[256:272] * y_last
            s1 = jnp.sum(inner, axis=0) + (edges[0] + edges[1])
            s2 = jnp.sum(inner * inner, axis=0) + (edges[0] * edges[0] + edges[1] * edges[1])
            if bz in (0, 16):
                s1, s2 = s1 * z_mask(bz), s2 * z_mask(bz)
            return s1, s2

        out = first_plane(1)
        pivot = sum_rows(out[16:256]) * (1.0 / 240.0)
        s1, s2 = plane_sums(1, out, pivot)
        for bz in range(17):
            if bz != 1:
                a1, a2 = plane_sums(bz, first_plane(bz), pivot)
                s1, s2 = s1 + a1, s2 + a2
        mean, inv = merge_stats(pivot, sum_rows(s1), sum_rows(s2))

        def normalise(bz, into, place):
            scale = inv * z_mask(bz)
            for by in range(17):
                here = scale * y_first if by == 0 else scale * y_last if by == 16 else scale
                v = leaky((raw[bz, 16 * by : 16 * by + 16] - mean) * here)
                even, odd = v[:, :128], v[:, 128:]
                before = jnp.where(row16 == 0, 0.0, pltpu.roll(odd, 1, 0))
                after = jnp.where(row16 == 15, 0.0, pltpu.roll(even, 15, 0))
                into[place, by] = jnp.concatenate([before, even, odd, after], axis=1).astype(BF16)

        def second_rows(held, first, rows):
            parts = [held[first + ez, ey : ey + rows].reshape(16 * rows, 512) for ey in range(2) for ez in range(2)]
            return jnp.concatenate(parts, axis=1)

        def second_pair(pair, held, pivot):
            lhs = jnp.concatenate([second_rows(held, 0, 16), second_rows(held, 1, 16)], axis=0)
            slabs = dot(lhs, second_ref[...])
            second[pl.ds(2 * pair, 2)] = slabs.reshape(2, 256, 256)
            d = (slabs - pivot).reshape(32, 16, 256)
            return jnp.sum(d, axis=0), jnp.sum(d * d, axis=0)

        for bz in range(3):
            normalise(bz, hidden_a, bz)
        pivot2 = sum_rows(dot(second_rows(hidden_a, 0, 8), second_ref[...])) * (1.0 / 128.0)

        def second_loop(i, sums):
            s1, s2 = sums
            for half, (held, later) in enumerate(((hidden_a, hidden_b), (hidden_b, hidden_a))):
                a1, a2 = second_pair(2 * i + half, held, pivot2)
                later[0] = held[2]
                for ahead in range(2):
                    normalise(jnp.minimum(4 * i + 2 * half + 3 + ahead, 16), later, 1 + ahead)
                s1, s2 = s1 + a1, s2 + a2
            return s1, s2

        zeros = jnp.zeros((16, 256), F32)
        s1, s2 = lax.fori_loop(0, 4, second_loop, (zeros, zeros))
        mean, inv = merge_stats(pivot2, sum_rows(s1), sum_rows(s2))

        logits = []
        for tz in range(2):
            parts, weights = [], []
            for b in range(8):
                h = leaky((second[8 * tz + b] - mean) * inv)
                top = h.astype(BF16)
                parts += [top, (h - top.astype(F32)).astype(BF16)]
                weights += [class_ref[b], class_ref[b]]
            logits.append(dot(jnp.concatenate(parts, axis=1), jnp.concatenate(weights, axis=0)))

        side = lax.broadcasted_iota(jnp.int32, (256, 128), 1) < 64
        t0, t1 = logits[0][:, 0:128], logits[0][:, 128:256]
        u0, u1 = logits[1][:, 0:128], logits[1][:, 128:256]
        l0 = jnp.where(side, t0, pltpu.roll(u0, 64, 1))
        l1 = jnp.where(side, pltpu.roll(t0, 64, 1), u0)
        l2 = jnp.where(side, t1, pltpu.roll(u1, 64, 1))
        most = jnp.maximum(jnp.maximum(l0, l1), l2)
        x0, x1, x2 = jnp.exp(l0 - most), jnp.exp(l1 - most), jnp.exp(l2 - most)
        share = blend_ref[...] / (x0 + x1 + x2)

        lane32 = lax.broadcasted_iota(jnp.int32, (64, 128), 1) // 32
        for k, x in enumerate((x0, x1)):
            w = (x * share).reshape(4, 4, 16, 128)
            sources = [w[:, r].reshape(64, 128) for r in range(4)]
            dest = []
            for q in range(4):
                got = None
                for r in range(4):
                    turn = (32 * (r - q)) % 128
                    piece = pltpu.roll(sources[r], turn, 1) if turn else sources[r]
                    got = piece if got is None else jnp.where(lane32 == r, piece, got)
                dest.append(got)
            for tx in range(2):
                for ty in range(2):
                    for h in range(2):
                        at = (2 * ty + h) * 16 + 8 * tx
                        for tz in range(2):
                            both = jnp.concatenate([dest[2 * tz][at : at + 8], dest[2 * tz + 1][at : at + 8]], axis=0)
                            rows = slice(16 * k, 16 * k + 16)
                            lanes = slice(128 * h, 128 * h + 128)
                            made[tx, slot, 2 * ty + tz, rows, lanes] = both.astype(BF16)
        return carry

    lax.fori_loop(0, plan_ref[0] + plan_ref[6] + plan_ref[7], patch, 0)
    low_out, ahead_out, right_low_out, right_up_out, left_up_out = outs
    low_out[...] = made[0, 0:3]
    ahead_out[0:3] = made[1, 0:3]
    ahead_out[3] = made[0, 6]
    right_low_out[...] = made[0, 3:6]
    right_up_out[...] = made[1, 3:6]
    left_up_out[0] = made[1, 6]


def network(plan, cubes, weights):
    def halves(count):
        return jax.ShapeDtypeStruct((count, 4, 16 * SENT, 256), BF16)

    return call(
        network_kernel,
        32,
        out_shape=(halves(3), halves(4), halves(3), halves(3), halves(1)),
        in_specs=[SMEM_SPEC] + [VMEM_SPEC] * 12,
        out_specs=(VMEM_SPEC,) * 5,
        scratch_shapes=[
            pltpu.VMEM((ENTRIES, 2, 4, 16, 256), BF16),
            pltpu.VMEM((2, ENTRIES, 4, 16 * SENT, 256), BF16),
            pltpu.VMEM((18, 16, 384), BF16),
            pltpu.VMEM((17, 272, 256), F32),
            pltpu.VMEM((3, 17, 16, 512), BF16),
            pltpu.VMEM((3, 17, 16, 512), BF16),
            pltpu.VMEM((16, 256, 256), F32),
        ],
        cost_estimate=pl.CostEstimate(flops=20_000_000_000, bytes_accessed=8_000_000, transcendentals=600_000),
        name="network",
    )(plan, *cubes, *weights)


def patch_entry(plan_ref, side, i):
    kept, right, left = [plan_ref[3 * side + j] for j in range(3)]
    if i < 3:
        return i < kept, jnp.int32(i)
    if i < 6:
        return i - 3 < right, jnp.minimum(kept + i - 3, HOME_MOST - 1)
    return left == 1, jnp.minimum(kept + right, HOME_MOST - 1)


def inverse_kernel(plan_ref, own_ref, prev_ref, parts_ref, inverse_ref, chosen_ref, chosen_parts):
    @pl.when(pl.program_id(0) == 0)
    def _():
        lane = lax.broadcasted_iota(jnp.int32, (1, 256), 1) % 64
        tiles = jnp.full((1, 256), -1, jnp.int32)
        for side, corner_ref in enumerate((own_ref, prev_ref)):
            for i in range(ENTRIES):
                live, slot = patch_entry(plan_ref, side, i)
                first = corner_ref[1, 0, slot] * TILES_Z + corner_ref[2, 0, slot]
                for t in range(4):
                    tile = jnp.where(live, first + TILES_Z * (t // 2) + t % 2, -1)
                    tiles = jnp.where(lane == 4 * (ENTRIES * side + i) + t, tile, tiles)
        same = lax.broadcasted_iota(jnp.int32, (256, 256), 0) == tiles
        hot = jnp.where(same, 1.0, 0.0).astype(BF16)
        chosen_parts[...] = hot
        chosen_ref[...] = hot[:, :128]

    weight = dot(chosen_parts[...], parts_ref[...])
    inverse_ref[...] = jnp.where(weight > 0, 1.0 / jnp.maximum(weight, 0.1), 0.0)


def inverse_weights(plan, corners, prev_corners):
    return call(
        inverse_kernel,
        12,
        grid=(4,),
        out_shape=(
            jax.ShapeDtypeStruct((TILES_Y * TILES_Z, TILE_VOX), F32),
            jax.ShapeDtypeStruct((TILES_Y * TILES_Z, 128), BF16),
        ),
        in_specs=[SMEM_SPEC] * 3 + [pl.BlockSpec((256, 1024), lambda i: (0, i))],
        out_specs=(pl.BlockSpec((256, 1024), lambda i: (0, i)), pl.BlockSpec((256, 128), lambda i: (0, 0))),
        scratch_shapes=[pltpu.VMEM((256, 256), BF16)],
        cost_estimate=pl.CostEstimate(flops=1_000_000_000, bytes_accessed=8_000_000, transcendentals=0),
        name="inverse_weights",
    )(plan, corners, prev_corners, jnp.asarray(blend_parts(), BF16))


def blend_kernel(
    plan_ref, chosen_ref, inverse_ref, low_ref, right_ref, ahead_ref, here_ref, across_ref, left_ref, out_ref, rows, stacked
):
    step = pl.program_id(0)

    @pl.when(step == 0)
    def _():
        for side in range(2):
            for i in range(ENTRIES):
                live, _ = patch_entry(plan_ref, side, i)
                number = 4 * (ENTRIES * side + i)
                if i < 3:
                    kept_ref = (low_ref, ahead_ref)[side]
                    sources = [(live, kept_ref, i)]
                elif i == 6:
                    sources = [(live, left_ref, 0) if side else (live, ahead_ref, 3)]
                elif side == 0:
                    sources = [(live, right_ref, i - 3)]
                else:
                    starts = plan_ref[8] == 1
                    sources = [
                        (live & jnp.logical_not(starts), here_ref, i - 3),
                        (live & starts, across_ref, i - 3),
                    ]
                for when, part_ref, place in sources:

                    @pl.when(when)
                    def _():
                        for t in range(4):
                            for h in range(2):
                                piece = part_ref[place, t, :, 128 * h : 128 * h + 128]
                                at = 40 * (number + t)
                                rows[h, at : at + 16 * SENT, :] = piece.astype(F32)

                @pl.when(jnp.logical_not(live))
                def _():
                    for h in range(2):
                        rows[h, 40 * number : 40 * number + 160, :] = jnp.zeros((160, 128), F32)

        blank = jnp.zeros((8, 128), F32)
        for x in range(16):
            for k in range(SENT):
                row = 16 * k + (x % 2) * 8 + x // 2
                for h in range(2):
                    for pair in range(4):
                        both = [rows[h, pl.ds(640 * pair + 320 * o + row, 8, stride=40), :] if 2 * pair + o < 7 else blank for o in range(2)]
                        at = 256 * k + 128 * h
                        stacked[x, 16 * pair : 16 * pair + 16, at : at + 128] = jnp.concatenate(both, axis=0).astype(BF16)

    for x in range(2):
        lanes = slice(256 * x, 256 * x + 256)
        inv = inverse_ref[:, lanes]
        got = dot(chosen_ref[:, 0:64], stacked[2 * step + x])
        p0, p1 = got[:, :256] * inv, got[:, 256:] * inv
        p2 = jnp.where(inv > 0, jnp.maximum(1.0 - p0 - p1, 0.0), 0.0)
        for k, p in enumerate((p0, p1, p2)):
            out_ref[:, k, :, lanes] = p.reshape(TILES_Y, TILES_Z, 256)


def blend(plan, chosen, inverse, *parts):
    return call(
        blend_kernel,
        16,
        grid=(8,),
        out_shape=jax.ShapeDtypeStruct((TILES_Y, CLASSES, TILES_Z, TILE_VOX), F32),
        in_specs=[SMEM_SPEC, VMEM_SPEC, pl.BlockSpec((256, 512), lambda i: (0, i))] + [VMEM_SPEC] * 6,
        out_specs=pl.BlockSpec((TILES_Y, CLASSES, TILES_Z, 512), lambda i: (0, 0, 0, i)),
        scratch_shapes=[
            pltpu.VMEM((2, 8 * ENTRIES * 40, 128), F32),
            pltpu.VMEM((16, 64, 256 * SENT), BF16),
        ],
        name="blend",
    )(plan, chosen, inverse, *parts)


def passed_along(block, axis, distance):
    devices = range(lax.axis_size(axis))
    route = [(i - distance, i) for i in devices if i - distance in devices]
    return lax.ppermute(block, axis, route)


def passed_round(block, distance):
    size = lax.axis_size("bal")
    return lax.ppermute(block, "bal", [(i, (i + distance) % size) for i in range(size)])


def passed_over(block, forward):
    axes = ("slab", "bal")
    members = lax.axis_size("bal")
    pairs = [(i, i + members) for i in range(0, lax.axis_size(axes) - members, members)]
    return lax.ppermute(block, axes, pairs if forward else [(b, a) for a, b in pairs])


def local(volume, first_kernel, second_kernel, class_weights, patch_corners, patch_counts):
    axes = ("slab", "bal")
    column = lax.axis_index(axes).astype(jnp.int32)
    corners = patch_corners.transpose(2, 0, 1)
    prev_corners = passed_along(corners, axes, 1)
    plan = make_plan(column[None], patch_counts)
    flat = flatten(volume[0])
    own_kept, own_right, own_left = gather_own(plan, corners, flat)
    right = passed_round(own_right, 1)
    back, here, two_back = gather_next(plan, prev_corners, flat, own_left)
    back = passed_along(back, axes, -1)
    across = passed_over(here, False)
    left = passed_along(two_back, axes, -2)
    weights = (
        jnp.asarray(select_x(), BF16),
        jnp.asarray(select_window(), BF16),
        *prepare_weights(first_kernel, second_kernel, class_weights),
        jnp.asarray(blend_rows(), F32),
    )
    low, ahead, right_low, right_up, left_up = network(plan, (own_kept, back, right, here, across, left), weights)
    ahead = passed_along(ahead, axes, 1)
    right_low = passed_round(right_low, -1)
    across_up = passed_over(right_up, True)
    left_up = passed_along(left_up, axes, 2)
    corners, prev_corners, low = lax.optimization_barrier((corners, prev_corners, low))
    inverse, chosen = inverse_weights(plan, corners, prev_corners)
    out = blend(plan, chosen, inverse, low, right_low, ahead, right_up, across_up, left_up)
    return out.transpose(0, 2, 1, 3)[None]


def solution(mesh):
    return jax.shard_map(
        local,
        mesh=mesh,
        in_specs=(
            P(("slab", "bal"), None, None, None),
            P(),
            P(),
            P(),
            P(("slab", "bal"), None, None),
            P(),
        ),
        out_specs=P(("slab", "bal"), None, None, None, None),
        check_vma=False,
    )
```

```python
import jax
import jax.numpy as jnp
import numpy as np
from jax import lax
from jax.experimental import pallas as pl
from jax.experimental.pallas import tpu as pltpu
from jax.sharding import PartitionSpec as P

PATCH = 32
HALF = 16
TILE_VOX = 4096
CHANNELS = 32
CLASSES = 3
ENTRIES = 7
SENT = 2
HOME_MOST = 6
TILES_Y = 4
TILES_Z = 64
F32 = jnp.float32
BF16 = jnp.bfloat16
MIB = 1024 * 1024


def select_x():
    out = np.zeros((4, 16, 32), np.float32)
    for wx in range(4):
        for bx in range(16):
            x = 2 * bx - 1 + wx
            if 0 <= x < 32:
                out[wx, bx, x] = 1
    return out.reshape(64, 32)


def select_window():
    out = np.zeros((4, 2, 2, 16, 3, 4, 2, 16), np.float32)
    for wx in range(4):
        for ypar in range(2):
            for g in range(3):
                for zw in range(16):
                    z = 12 * g - 2 + zw
                    if 0 <= z < 32:
                        out[wx, z // 16, ypar, z % 16, g, wx, ypar, zw] = 1
    return out.reshape(256, 384)


def blend_map():
    coordinate = np.arange(PATCH, dtype=np.float32)
    square = (coordinate - np.float32(15.5)) ** 2 / np.float32(32.0)
    total = square[:, None, None] + square[None, :, None] + square[None, None, :]
    return (np.float32(0.1) + np.float32(0.9) * np.exp(-total)).astype(np.float32)


def blend_rows():
    b = blend_map().reshape(16, 2, 16, 2, 2, 16)
    return b.transpose(2, 0, 4, 1, 3, 5).reshape(256, 128)


def blend_parts():
    b = blend_map().reshape(2, 16, 2, 16, 2, 16).transpose(0, 2, 4, 1, 3, 5).reshape(2, 4, TILE_VOX)
    out = np.zeros((4, 64, TILE_VOX), np.float32)
    for side in range(2):
        for patch in range(ENTRIES):
            at = 4 * (ENTRIES * side + patch)
            rest = b[side]
            for part in range(3):
                top = rest.astype(jnp.bfloat16).astype(np.float32)
                out[part, at : at + 4] = top
                rest = rest - top
    return out.reshape(256, TILE_VOX)


def call(kernel, vmem, **options):
    params = pltpu.CompilerParams(vmem_limit_bytes=vmem * MIB)
    return pl.pallas_call(kernel, compiler_params=params, **options)


SMEM_SPEC = pl.BlockSpec(memory_space=pltpu.SMEM)
VMEM_SPEC = pl.BlockSpec(memory_space=pltpu.VMEM)


def write_plan(column_ref, count_ref, plan_ref, sent):
    column = column_ref[0]

    def group_plan(group, at):
        heavy = jnp.int32(0)
        for i in (3, 2, 1, 0):
            heavy = jnp.where(count_ref[4 * group + i] == HOME_MOST, i, heavy)
        place = [(heavy + k) % 4 for k in range(4)]
        count = [count_ref[4 * group + place[k]] for k in range(4)]
        left = [jnp.where((count[1] >= 4) & (heavy >= 1), 1, 0), 0, 0, 0]
        right = []
        coming = 0
        for k in range(4):
            load = count[k] + coming - left[k]
            if k == 3:
                load = load + left[0]
                left[3] = jnp.where((load > 3) & (place[3] >= 1), 1, 0)
                load = load - left[3]
            out = jnp.clip(load - 3, 0, jnp.minimum(count[k] - left[k], 3))
            right.append(out)
            coming = out
        for k in range(4):
            sent[at + place[k]] = right[k]
            sent[at + 4 + place[k]] = left[k]

    def column_plan(where, at, out):
        me = where % 4
        right, left = sent[at + me], sent[at + 4 + me]
        plan_ref[out] = count_ref[where] - right - left
        plan_ref[out + 1] = right
        plan_ref[out + 2] = left

    group_plan(column // 4, 0)
    column_plan(column, 0, 0)
    me = column % 4
    plan_ref[6] = sent[(me + 3) % 4]
    plan_ref[7] = jnp.where(me == 3, 0, sent[4 + (me + 1) % 4])
    plan_ref[8] = jnp.where(me == 0, 1, 0)
    before = jnp.maximum(column - 1, 0)
    group_plan(before // 4, 8)
    column_plan(before, 8, 3)

    @pl.when(column == 0)
    def _():
        for i in range(3):
            plan_ref[3 + i] = 0


def flatten(volume_ref, copies, flat):
    for ty in range(TILES_Y):
        copies[ty].wait()
        for group in range(TILES_Z // 16):
            for lane_tile in range(32):
                block = volume_ref[ty, 16 * group : 16 * group + 16, 128 * lane_tile : 128 * lane_tile + 128].astype(F32)
                for half in range(2):
                    start = ((ty * 8 + 2 * group + half) * 32 + lane_tile) * 8
                    flat[start : start + 8, :] = block[8 * half : 8 * half + 8]


def take_tiles(corner_ref, flat, out_ref, slot, place):
    for tile in range(4):
        ty = corner_ref[1, 0, slot] + tile // 2
        tz = corner_ref[2, 0, slot] + tile % 2
        base = (ty * 8 + tz // 8) * 256 + tz % 8
        rows = []
        for x_half in range(2):
            parts = [flat[pl.ds(base + 128 * x_half + 8 * h, 8, stride=16), :] for h in range(2)]
            rows.append(jnp.concatenate(parts, axis=1))
        out_ref[place, tile] = jnp.concatenate(rows, axis=0).astype(BF16)


def take_entries(plan_ref, at, corner_ref, flat, kept_out, right_out, left_out):
    kept, right = plan_ref[at], plan_ref[at + 1]

    @pl.loop(0, kept)
    def _(slot):
        take_tiles(corner_ref, flat, kept_out, slot, slot)

    @pl.loop(0, right)
    def _(slot):
        take_tiles(corner_ref, flat, right_out, kept + slot, slot)

    @pl.when(plan_ref[at + 2] == 1)
    def _():
        take_tiles(corner_ref, flat, left_out, kept + right, 0)


def gather_kernel(
    column_ref, prev_ref, count_hbm, own_hbm, volume_hbm,
    plan_ref, kept_out, right_out, back_out, here_out, two_back_out,
    flat, own_left, sent, count_ref, own_ref, volume_ref, arrived,
):
    count_copy = pltpu.make_async_copy(count_hbm, count_ref, arrived.at[4])
    own_copy = pltpu.make_async_copy(own_hbm, own_ref, arrived.at[5])
    copies = [pltpu.make_async_copy(volume_hbm.at[ty], volume_ref.at[ty], arrived.at[ty]) for ty in range(TILES_Y)]
    for copy in [count_copy, own_copy] + copies:
        copy.start()
    count_copy.wait()
    write_plan(column_ref, count_ref, plan_ref, sent)
    own_copy.wait()
    flatten(volume_ref, copies, flat)
    take_entries(plan_ref, 0, own_ref, flat, kept_out, right_out, own_left)
    take_entries(plan_ref, 3, prev_ref, flat, back_out, here_out, two_back_out)
    back_out[3] = own_left[0]


def gather(column, patch_counts, corners, prev_corners, volume):
    def tiles(count):
        return jax.ShapeDtypeStruct((count, 4, 16, 256), BF16)

    return call(
        gather_kernel,
        58,
        out_shape=(jax.ShapeDtypeStruct((9,), jnp.int32), tiles(3), tiles(3), tiles(4), tiles(3), tiles(1)),
        in_specs=[SMEM_SPEC] * 2 + [pl.BlockSpec(memory_space=pltpu.HBM)] * 3,
        out_specs=(SMEM_SPEC,) + (VMEM_SPEC,) * 5,
        scratch_shapes=[
            pltpu.VMEM((TILES_Y * TILES_Z * 32, 128), F32),
            pltpu.VMEM((1, 4, 16, 256), BF16),
            pltpu.SMEM((16,), jnp.int32),
            pltpu.SMEM(patch_counts.shape, jnp.int32),
            pltpu.SMEM(corners.shape, jnp.int32),
            pltpu.VMEM((TILES_Y, TILES_Z, TILE_VOX), BF16),
            pltpu.SemaphoreType.DMA((6,)),
        ],
        name="gather",
    )(column, prev_corners, patch_counts, corners, volume)


def dot(a, b):
    return jnp.dot(a, b, preferred_element_type=F32)


def weights_kernel(first_ref, second_ref, class_ref, first_out, second_out, class_out, four, taps, turned):
    lane = lax.broadcasted_iota(jnp.int32, (32, 256), 1)
    taps[...] = jnp.zeros((32, 32), F32)
    for dx in range(3):
        for dy in range(3):
            at = 9 * dx + 3 * dy
            taps[at : at + 3, :] = first_ref[dx, dy].astype(F32)
    first = jnp.concatenate([taps[...]] * 8, axis=1)
    big = jnp.concatenate([jnp.where(lane // 32 == s, first, 0.0).astype(BF16) for s in range(8)], axis=0)
    row = lax.broadcasted_iota(jnp.int32, (256, 256), 0)
    col = lax.broadcasted_iota(jnp.int32, (256, 256), 1)
    tap = col % 32
    dx = jnp.where(tap >= 18, 2, jnp.where(tap >= 9, 1, 0))
    rest = tap - 9 * dx
    dy = jnp.where(rest >= 6, 2, jnp.where(rest >= 3, 1, 0))
    dz = rest - 3 * dy
    fits = ((row // 32) % 4 == col // 128 + dx) & (row // 128 * 2 + (row // 16) % 2 == (col // 64) % 2 + dy) & (tap < 27)
    ahead = row % 16 - (col // 32) % 2 - dz
    for j in range(6):
        spread = jnp.where(fits & (ahead == 2 * j), 1.0, 0.0).astype(BF16)
        first_out[j] = dot(spread, big).astype(BF16)

    part = lax.broadcasted_iota(jnp.int32, (32, 128), 1) // 32
    for tap in range(27):
        four[tap] = jnp.concatenate([second_ref[tap].astype(F32)] * 4, axis=1)
    for qx in range(4):
        for qy in range(4):
            for qz in range(4):
                at = ((((qy // 2 * 2 + qz // 2) * 2 + qx // 2) * 2 + qx % 2) * 2 + qy % 2) * 2 + qz % 2
                for half in range(2):
                    got = jnp.zeros((32, 128), F32)
                    for s in range(4):
                        dx, dy, dz = qx - half, qy - s // 2, qz - s % 2
                        if min(dx, dy, dz) >= 0 and max(dx, dy, dz) <= 2:
                            got = jnp.where(part == s, four[(dx * 3 + dy) * 3 + dz], got)
                    second_out[32 * at : 32 * at + 32, 128 * half : 128 * half + 128] = got.astype(BF16)

    turned[...] = jnp.zeros((128, 128), F32)
    turned[0:CLASSES, 0:CHANNELS] = class_ref[...].astype(F32)
    classes = turned[...].T
    columns = jnp.zeros((32, 256), F32)
    for k in range(CLASSES):
        columns = jnp.where(lane // 64 == k, classes[0:32, k : k + 1], columns)
    for b in range(8):
        for s in range(8):
            place = 32 * (s // 4) + 16 * (s // 2 % 2) + 2 * b + s % 2
            class_out[b, 32 * s : 32 * s + 32, :] = jnp.where(lane % 64 == place, columns, 0.0).astype(BF16)


def prepare_weights(first_kernel, second_kernel, class_weights):
    return call(
        weights_kernel,
        12,
        out_shape=(
            jax.ShapeDtypeStruct((6, 256, 256), BF16),
            jax.ShapeDtypeStruct((2048, 256), BF16),
            jax.ShapeDtypeStruct((8, 256, 256), BF16),
        ),
        in_specs=[VMEM_SPEC] * 3,
        out_specs=(VMEM_SPEC,) * 3,
        scratch_shapes=[pltpu.VMEM((27, 32, 128), F32), pltpu.VMEM((32, 32), F32), pltpu.VMEM((128, 128), F32)],
        cost_estimate=pl.CostEstimate(flops=1_000_000_000, bytes_accessed=8_000_000, transcendentals=0),
        name="weights",
    )(first_kernel, second_kernel.reshape(27, CHANNELS, CHANNELS), class_weights.T)


def fold_channels(row):
    half = row[:, :128] + row[:, 128:]
    half = half + pltpu.roll(half, 64, 1)
    half = half + pltpu.roll(half, 32, 1)
    return jnp.concatenate([half, half], axis=1)


def merge_stats(pivot, s1, s2):
    count = 4096.0
    lane_mean = pivot + s1 * (1.0 / count)
    lane_m2 = s2 - s1 * s1 * (1.0 / count)
    mean = fold_channels(lane_mean) * 0.125
    off = lane_mean - mean
    var = fold_channels(lane_m2 + count * (off * off)) * (1.0 / 32768.0)
    return mean, lax.rsqrt(var + 1e-05)


def leaky(v):
    return jnp.maximum(v, 0.01 * v)


def sum_rows(block):
    return jnp.sum(block, axis=0, keepdims=True)


def network_kernel(plan_ref, own_ref, back_ref, right_ref, here_ref, across_ref, left_ref, *refs):
    pick_ref, window_ref, first_ref, second_ref, class_ref, blend_ref = refs[:6]
    outs, (cubes, made, spread, raw, hidden_a, hidden_b, second) = refs[6:-7], refs[-7:]
    for i in range(3):
        cubes[i, 0] = own_ref[i]
        cubes[i, 1] = back_ref[i]
        cubes[3 + i, 0] = right_ref[i]
    cubes[6, 0] = back_ref[3]
    cubes[6, 1] = left_ref[0]

    @pl.when(plan_ref[8] == 0)
    def _():
        for i in range(3):
            cubes[3 + i, 1] = here_ref[i]

    @pl.when(plan_ref[8] == 1)
    def _():
        for i in range(3):
            cubes[3 + i, 1] = across_ref[i]

    spread[0] = jnp.zeros((16, 384), BF16)
    spread[17] = jnp.zeros((16, 384), BF16)
    lane = lax.broadcasted_iota(jnp.int32, (1, 256), 1)
    sy, sz = (lane % 128) // 64, (lane % 64) // 32
    y_first = (sy == 1).astype(F32)
    y_last = (sy == 0).astype(F32)
    row16 = lax.broadcasted_iota(jnp.int32, (16, 128), 0)
    lane16 = lax.broadcasted_iota(jnp.int32, (16, 128), 1) // 32

    def z_mask(bz):
        bad = ((bz == 0) & (sz == 0)) | ((bz == 16) & (sz == 1))
        return jnp.where(bad, 0.0, 1.0)

    def patch(index, carry):
        kept = plan_ref[0]
        later = jnp.where(index - kept < plan_ref[6], 3 + index - kept, 6)
        slot = jnp.where(index < kept, index, later)
        cube = jnp.concatenate(
            [jnp.concatenate([cubes[slot, tx, t] for t in range(4)], axis=1) for tx in range(2)], axis=0
        )
        moved = dot(pick_ref[...], cube)
        lists = []
        for ty in range(2):
            for quad in range(2):
                pieces = []
                for wx in range(4):
                    for tz in range(2):
                        at = (ty * 2 + tz) * 256 + quad * 128
                        pieces.append(moved[16 * wx : 16 * wx + 16, at : at + 128])
                for r in range(4):
                    joined = []
                    for tile in range(2):
                        got = None
                        for place in range(4):
                            piece = pieces[4 * tile + place]
                            turn = (32 * (place - r)) % 128
                            if turn:
                                piece = pltpu.roll(piece, turn, 1)
                            got = piece if got is None else jnp.where(lane16 == place, piece, got)
                        joined.append(got)
                    lists.append(jnp.concatenate(joined, axis=1).astype(BF16))
        rows = jnp.concatenate(lists, axis=0)
        spread[1:17] = dot(rows, window_ref[...]).astype(BF16).reshape(16, 16, 384)

        def first_plane(bz):
            lanes = slice(128 * (bz // 6), 128 * (bz // 6) + 128)
            lhs = jnp.concatenate([spread[0:17, :, lanes], spread[1:18, :, lanes]], axis=2).reshape(272, 256)
            out = dot(lhs, first_ref[bz % 6])
            raw[bz] = out
            return out

        def plane_sums(bz, out, pivot):
            d = out - pivot
            inner = d[16:256].reshape(15, 16, 256)
            edges = d[0:16] * y_first, d[256:272] * y_last
            s1 = jnp.sum(inner, axis=0) + (edges[0] + edges[1])
            s2 = jnp.sum(inner * inner, axis=0) + (edges[0] * edges[0] + edges[1] * edges[1])
            if bz in (0, 16):
                s1, s2 = s1 * z_mask(bz), s2 * z_mask(bz)
            return s1, s2

        out = first_plane(1)
        pivot = sum_rows(out[16:256]) * (1.0 / 240.0)
        s1, s2 = plane_sums(1, out, pivot)
        for bz in range(17):
            if bz != 1:
                a1, a2 = plane_sums(bz, first_plane(bz), pivot)
                s1, s2 = s1 + a1, s2 + a2
        mean, inv = merge_stats(pivot, sum_rows(s1), sum_rows(s2))

        def normalise(bz, into, place):
            scale = inv * z_mask(bz)
            for by in range(17):
                here = scale * y_first if by == 0 else scale * y_last if by == 16 else scale
                v = leaky((raw[bz, 16 * by : 16 * by + 16] - mean) * here)
                even, odd = v[:, :128], v[:, 128:]
                before = jnp.where(row16 == 0, 0.0, pltpu.roll(odd, 1, 0))
                after = jnp.where(row16 == 15, 0.0, pltpu.roll(even, 15, 0))
                into[place, by] = jnp.concatenate([before, even, odd, after], axis=1).astype(BF16)

        def second_rows(held, first, rows):
            parts = [held[first + ez, ey : ey + rows].reshape(16 * rows, 512) for ey in range(2) for ez in range(2)]
            return jnp.concatenate(parts, axis=1)

        def second_four(four, held, pivot):
            lhs = jnp.concatenate([second_rows(held, i, 16) for i in range(4)], axis=0)
            slabs = dot(lhs, second_ref[...])
            second[pl.ds(4 * four, 4)] = slabs.reshape(4, 256, 256)
            d = (slabs - pivot).reshape(64, 16, 256)
            return jnp.sum(d, axis=0), jnp.sum(d * d, axis=0)

        for bz in range(5):
            normalise(bz, hidden_a, bz)
        pivot2 = sum_rows(dot(second_rows(hidden_a, 0, 8), second_ref[...])) * (1.0 / 128.0)

        def second_loop(i, sums):
            s1, s2 = sums
            for half, (held, later) in enumerate(((hidden_a, hidden_b), (hidden_b, hidden_a))):
                a1, a2 = second_four(2 * i + half, held, pivot2)
                later[0] = held[4]
                for ahead in range(4):
                    normalise(jnp.minimum(8 * i + 4 * half + 5 + ahead, 16), later, 1 + ahead)
                s1, s2 = s1 + a1, s2 + a2
            return s1, s2

        zeros = jnp.zeros((16, 256), F32)
        s1, s2 = lax.fori_loop(0, 2, second_loop, (zeros, zeros))
        mean, inv = merge_stats(pivot2, sum_rows(s1), sum_rows(s2))

        logits = []
        for tz in range(2):
            parts, weights = [], []
            for b in range(8):
                h = leaky((second[8 * tz + b] - mean) * inv)
                top = h.astype(BF16)
                parts += [top, (h - top.astype(F32)).astype(BF16)]
                weights += [class_ref[b], class_ref[b]]
            logits.append(dot(jnp.concatenate(parts, axis=1), jnp.concatenate(weights, axis=0)))

        side = lax.broadcasted_iota(jnp.int32, (256, 128), 1) < 64
        t0, t1 = logits[0][:, 0:128], logits[0][:, 128:256]
        u0, u1 = logits[1][:, 0:128], logits[1][:, 128:256]
        l0 = jnp.where(side, t0, pltpu.roll(u0, 64, 1))
        l1 = jnp.where(side, pltpu.roll(t0, 64, 1), u0)
        l2 = jnp.where(side, t1, pltpu.roll(u1, 64, 1))
        most = jnp.maximum(jnp.maximum(l0, l1), l2)
        x0, x1, x2 = jnp.exp(l0 - most), jnp.exp(l1 - most), jnp.exp(l2 - most)
        share = blend_ref[...] / (x0 + x1 + x2)

        lane32 = lax.broadcasted_iota(jnp.int32, (64, 128), 1) // 32
        for k, x in enumerate((x0, x1)):
            w = (x * share).reshape(4, 4, 16, 128)
            sources = [w[:, r].reshape(64, 128) for r in range(4)]
            dest = []
            for q in range(4):
                got = None
                for r in range(4):
                    turn = (32 * (r - q)) % 128
                    piece = pltpu.roll(sources[r], turn, 1) if turn else sources[r]
                    got = piece if got is None else jnp.where(lane32 == r, piece, got)
                dest.append(got)
            for tx in range(2):
                for ty in range(2):
                    for h in range(2):
                        at = (2 * ty + h) * 16 + 8 * tx
                        for tz in range(2):
                            both = jnp.concatenate([dest[2 * tz][at : at + 8], dest[2 * tz + 1][at : at + 8]], axis=0)
                            rows = slice(16 * k, 16 * k + 16)
                            lanes = slice(128 * h, 128 * h + 128)
                            made[tx, slot, 2 * ty + tz, rows, lanes] = both.astype(BF16)
        return carry

    lax.fori_loop(0, plan_ref[0] + plan_ref[6] + plan_ref[7], patch, 0)
    low_out, ahead_out, right_low_out, right_up_out, left_up_out = outs
    low_out[...] = made[0, 0:3]
    ahead_out[0:3] = made[1, 0:3]
    ahead_out[3] = made[0, 6]
    right_low_out[...] = made[0, 3:6]
    right_up_out[...] = made[1, 3:6]
    left_up_out[0] = made[1, 6]


def network(plan, cubes, weights):
    def halves(count):
        return jax.ShapeDtypeStruct((count, 4, 16 * SENT, 256), BF16)

    return call(
        network_kernel,
        32,
        out_shape=(halves(3), halves(4), halves(3), halves(3), halves(1)),
        in_specs=[SMEM_SPEC] + [VMEM_SPEC] * 12,
        out_specs=(VMEM_SPEC,) * 5,
        scratch_shapes=[
            pltpu.VMEM((ENTRIES, 2, 4, 16, 256), BF16),
            pltpu.VMEM((2, ENTRIES, 4, 16 * SENT, 256), BF16),
            pltpu.VMEM((18, 16, 384), BF16),
            pltpu.VMEM((17, 272, 256), F32),
            pltpu.VMEM((5, 17, 16, 512), BF16),
            pltpu.VMEM((5, 17, 16, 512), BF16),
            pltpu.VMEM((16, 256, 256), F32),
        ],
        cost_estimate=pl.CostEstimate(flops=20_000_000_000, bytes_accessed=8_000_000, transcendentals=600_000),
        name="network",
    )(plan, *cubes, *weights)


def patch_entry(plan_ref, side, i):
    kept, right, left = [plan_ref[3 * side + j] for j in range(3)]
    if i < 3:
        return i < kept, jnp.int32(i)
    if i < 6:
        return i - 3 < right, jnp.minimum(kept + i - 3, HOME_MOST - 1)
    return left == 1, jnp.minimum(kept + right, HOME_MOST - 1)


def inverse_kernel(plan_ref, own_ref, prev_ref, parts_ref, inverse_ref, chosen_ref, chosen_parts):
    @pl.when(pl.program_id(0) == 0)
    def _():
        lane = lax.broadcasted_iota(jnp.int32, (1, 256), 1) % 64
        tiles = jnp.full((1, 256), -1, jnp.int32)
        for side, corner_ref in enumerate((own_ref, prev_ref)):
            for i in range(ENTRIES):
                live, slot = patch_entry(plan_ref, side, i)
                first = corner_ref[1, 0, slot] * TILES_Z + corner_ref[2, 0, slot]
                for t in range(4):
                    tile = jnp.where(live, first + TILES_Z * (t // 2) + t % 2, -1)
                    tiles = jnp.where(lane == 4 * (ENTRIES * side + i) + t, tile, tiles)
        same = lax.broadcasted_iota(jnp.int32, (256, 256), 0) == tiles
        hot = jnp.where(same, 1.0, 0.0).astype(BF16)
        chosen_parts[...] = hot
        chosen_ref[...] = hot[:, :128]

    weight = dot(chosen_parts[...], parts_ref[...])
    inverse_ref[...] = jnp.where(weight > 0, 1.0 / jnp.maximum(weight, 0.1), 0.0)


def inverse_weights(plan, corners, prev_corners):
    return call(
        inverse_kernel,
        12,
        grid=(4,),
        out_shape=(
            jax.ShapeDtypeStruct((TILES_Y * TILES_Z, TILE_VOX), F32),
            jax.ShapeDtypeStruct((TILES_Y * TILES_Z, 128), BF16),
        ),
        in_specs=[SMEM_SPEC] * 3 + [pl.BlockSpec((256, 1024), lambda i: (0, i))],
        out_specs=(pl.BlockSpec((256, 1024), lambda i: (0, i)), pl.BlockSpec((256, 128), lambda i: (0, 0))),
        scratch_shapes=[pltpu.VMEM((256, 256), BF16)],
        cost_estimate=pl.CostEstimate(flops=1_000_000_000, bytes_accessed=8_000_000, transcendentals=0),
        name="inverse_weights",
    )(plan, corners, prev_corners, jnp.asarray(blend_parts(), BF16))


def blend_kernel(
    plan_ref, chosen_ref, inverse_ref, low_ref, right_ref, ahead_ref, here_ref, across_ref, left_ref, out_ref, rows, stacked, staged, written
):
    for side in range(2):
        for i in range(ENTRIES):
            live, _ = patch_entry(plan_ref, side, i)
            number = 4 * (ENTRIES * side + i)
            if i < 3:
                kept_ref = (low_ref, ahead_ref)[side]
                sources = [(live, kept_ref, i)]
            elif i == 6:
                sources = [(live, left_ref, 0) if side else (live, ahead_ref, 3)]
            elif side == 0:
                sources = [(live, right_ref, i - 3)]
            else:
                starts = plan_ref[8] == 1
                sources = [
                    (live & jnp.logical_not(starts), here_ref, i - 3),
                    (live & starts, across_ref, i - 3),
                ]
            for when, part_ref, place in sources:

                @pl.when(when)
                def _():
                    for t in range(4):
                        for h in range(2):
                            piece = part_ref[place, t, :, 128 * h : 128 * h + 128]
                            at = 40 * (number + t)
                            rows[h, at : at + 16 * SENT, :] = piece.astype(F32)

            @pl.when(jnp.logical_not(live))
            def _():
                for h in range(2):
                    rows[h, 40 * number : 40 * number + 160, :] = jnp.zeros((160, 128), F32)

    blank = jnp.zeros((8, 128), F32)
    for x in range(16):
        for k in range(SENT):
            row = 16 * k + (x % 2) * 8 + x // 2
            for h in range(2):
                for pair in range(4):
                    both = [rows[h, pl.ds(640 * pair + 320 * o + row, 8, stride=40), :] if 2 * pair + o < 7 else blank for o in range(2)]
                    at = 256 * k + 128 * h
                    stacked[x, 16 * pair : 16 * pair + 16, at : at + 128] = jnp.concatenate(both, axis=0).astype(BF16)

    def part_copy(x):
        lanes = pl.ds(pl.multiple_of(256 * x, 256), 256)
        return pltpu.make_async_copy(staged.at[:, :, :, lanes], out_ref.at[:, :, :, lanes], written.at[x])

    @pl.loop(0, 16)
    def _(x):
        lanes = pl.ds(pl.multiple_of(256 * x, 256), 256)
        inv = inverse_ref[:, lanes]
        got = dot(chosen_ref[:, 0:64], stacked[x])
        p0, p1 = got[:, :256] * inv, got[:, 256:] * inv
        p2 = jnp.where(inv > 0, jnp.maximum(1.0 - p0 - p1, 0.0), 0.0)
        for k, p in enumerate((p0, p1, p2)):
            staged[:, k, :, lanes] = p.reshape(TILES_Y, TILES_Z, 256)
        part_copy(x).start()

    @pl.loop(0, 16)
    def _(x):
        part_copy(x).wait()


def blend(plan, chosen, inverse, *parts):
    shape = (TILES_Y, CLASSES, TILES_Z, TILE_VOX)
    return call(
        blend_kernel,
        28,
        out_shape=jax.ShapeDtypeStruct(shape, F32),
        in_specs=[SMEM_SPEC] + [VMEM_SPEC] * 8,
        out_specs=pl.BlockSpec(memory_space=pl.ANY),
        scratch_shapes=[
            pltpu.VMEM((2, 8 * ENTRIES * 40, 128), F32),
            pltpu.VMEM((16, 64, 256 * SENT), BF16),
            pltpu.VMEM(shape, F32),
            pltpu.SemaphoreType.DMA((16,)),
        ],
        name="blend",
    )(plan, chosen, inverse, *parts)


def passed_along(block, axis, distance):
    devices = range(lax.axis_size(axis))
    route = [(i - distance, i) for i in devices if i - distance in devices]
    return lax.ppermute(block, axis, route)


def passed_round(block, distance):
    size = lax.axis_size("bal")
    return lax.ppermute(block, "bal", [(i, (i + distance) % size) for i in range(size)])


def passed_over(block, forward):
    axes = ("slab", "bal")
    members = lax.axis_size("bal")
    pairs = [(i, i + members) for i in range(0, lax.axis_size(axes) - members, members)]
    return lax.ppermute(block, axes, pairs if forward else [(b, a) for a, b in pairs])


def local(volume, first_kernel, second_kernel, class_weights, patch_corners, patch_counts):
    axes = ("slab", "bal")
    column = lax.axis_index(axes).astype(jnp.int32)
    corners = patch_corners.transpose(2, 0, 1)
    prev_corners = passed_along(corners, axes, 1)
    plan, own_kept, own_right, back, here, two_back = gather(column[None], patch_counts, corners, prev_corners, volume[0])
    right = passed_round(own_right, 1)
    back = passed_along(back, axes, -1)
    across = passed_over(here, False)
    left = passed_along(two_back, axes, -2)
    weights = (
        jnp.asarray(select_x(), BF16),
        jnp.asarray(select_window(), BF16),
        *prepare_weights(first_kernel, second_kernel, class_weights),
        jnp.asarray(blend_rows(), F32),
    )
    low, ahead, right_low, right_up, left_up = network(plan, (own_kept, back, right, here, across, left), weights)
    ahead = passed_along(ahead, axes, 1)
    right_low = passed_round(right_low, -1)
    across_up = passed_over(right_up, True)
    left_up = passed_along(left_up, axes, 2)
    corners, prev_corners, low = lax.optimization_barrier((corners, prev_corners, low))
    inverse, chosen = inverse_weights(plan, corners, prev_corners)
    out = blend(plan, chosen, inverse, low, right_low, ahead, right_up, across_up, left_up)
    return out.transpose(0, 2, 1, 3)[None]


def solution(mesh):
    return jax.shard_map(
        local,
        mesh=mesh,
        in_specs=(
            P(("slab", "bal"), None, None, None),
            P(),
            P(),
            P(),
            P(("slab", "bal"), None, None),
            P(),
        ),
        out_specs=P(("slab", "bal"), None, None, None, None),
        check_vma=False,
    )
```

```python
import jax
import jax.numpy as jnp
import numpy as np
from jax import lax
from jax.experimental import pallas as pl
from jax.experimental.pallas import tpu as pltpu
from jax.sharding import PartitionSpec as P

PATCH = 32
HALF = 16
TILE_VOX = 4096
CHANNELS = 32
CLASSES = 3
ENTRIES = 7
SENT = 2
HOME_MOST = 6
TILES_Y = 4
TILES_Z = 64
F32 = jnp.float32
BF16 = jnp.bfloat16
MIB = 1024 * 1024


def select_x():
    out = np.zeros((4, 16, 32), np.float32)
    for wx in range(4):
        for bx in range(16):
            x = 2 * bx - 1 + wx
            if 0 <= x < 32:
                out[wx, bx, x] = 1
    return out.reshape(64, 32)


def select_window():
    out = np.zeros((4, 2, 2, 16, 3, 4, 2, 16), np.float32)
    for wx in range(4):
        for ypar in range(2):
            for g in range(3):
                for zw in range(16):
                    z = 12 * g - 2 + zw
                    if 0 <= z < 32:
                        out[wx, z // 16, ypar, z % 16, g, wx, ypar, zw] = 1
    return out.reshape(256, 384)


def blend_map():
    coordinate = np.arange(PATCH, dtype=np.float32)
    square = (coordinate - np.float32(15.5)) ** 2 / np.float32(32.0)
    total = square[:, None, None] + square[None, :, None] + square[None, None, :]
    return (np.float32(0.1) + np.float32(0.9) * np.exp(-total)).astype(np.float32)


def blend_rows():
    b = blend_map().reshape(16, 2, 16, 2, 2, 16)
    return b.transpose(2, 0, 4, 1, 3, 5).reshape(256, 128)


def blend_parts():
    b = blend_map().reshape(2, 16, 2, 16, 2, 16).transpose(0, 2, 4, 1, 3, 5).reshape(2, 4, TILE_VOX)
    out = np.zeros((4, 64, TILE_VOX), np.float32)
    for side in range(2):
        for patch in range(ENTRIES):
            at = 4 * (ENTRIES * side + patch)
            rest = b[side]
            for part in range(3):
                top = rest.astype(jnp.bfloat16).astype(np.float32)
                out[part, at : at + 4] = top
                rest = rest - top
    return out.reshape(256, TILE_VOX)


def call(kernel, vmem, **options):
    params = pltpu.CompilerParams(vmem_limit_bytes=vmem * MIB)
    return pl.pallas_call(kernel, compiler_params=params, **options)


SMEM_SPEC = pl.BlockSpec(memory_space=pltpu.SMEM)
VMEM_SPEC = pl.BlockSpec(memory_space=pltpu.VMEM)


def write_plan(column_ref, count_ref, plan_ref, sent):
    column = column_ref[0]

    def group_plan(group, at):
        heavy = jnp.int32(0)
        for i in (3, 2, 1, 0):
            heavy = jnp.where(count_ref[4 * group + i] == HOME_MOST, i, heavy)
        place = [(heavy + k) % 4 for k in range(4)]
        count = [count_ref[4 * group + place[k]] for k in range(4)]
        left = [jnp.where((count[1] >= 4) & (heavy >= 1), 1, 0), 0, 0, 0]
        right = []
        coming = 0
        for k in range(4):
            load = count[k] + coming - left[k]
            if k == 3:
                load = load + left[0]
                left[3] = jnp.where((load > 3) & (place[3] >= 1), 1, 0)
                load = load - left[3]
            out = jnp.clip(load - 3, 0, jnp.minimum(count[k] - left[k], 3))
            right.append(out)
            coming = out
        for k in range(4):
            sent[at + place[k]] = right[k]
            sent[at + 4 + place[k]] = left[k]

    def column_plan(where, at, out):
        me = where % 4
        right, left = sent[at + me], sent[at + 4 + me]
        plan_ref[out] = count_ref[where] - right - left
        plan_ref[out + 1] = right
        plan_ref[out + 2] = left

    group_plan(column // 4, 0)
    column_plan(column, 0, 0)
    me = column % 4
    plan_ref[6] = sent[(me + 3) % 4]
    plan_ref[7] = jnp.where(me == 3, 0, sent[4 + (me + 1) % 4])
    plan_ref[8] = jnp.where(me == 0, 1, 0)
    before = jnp.maximum(column - 1, 0)
    group_plan(before // 4, 8)
    column_plan(before, 8, 3)

    @pl.when(column == 0)
    def _():
        for i in range(3):
            plan_ref[3 + i] = 0


def flatten(volume_ref, copies, flat):
    for ty in range(TILES_Y):
        copies[ty].wait()
        for group in range(TILES_Z // 16):
            for lane_tile in range(32):
                block = volume_ref[ty, 16 * group : 16 * group + 16, 128 * lane_tile : 128 * lane_tile + 128].astype(F32)
                for half in range(2):
                    start = ((ty * 8 + 2 * group + half) * 32 + lane_tile) * 8
                    flat[start : start + 8, :] = block[8 * half : 8 * half + 8]


def take_tiles(corner_ref, flat, out_ref, slot, place):
    for tile in range(4):
        ty = corner_ref[1, 0, slot] + tile // 2
        tz = corner_ref[2, 0, slot] + tile % 2
        base = (ty * 8 + tz // 8) * 256 + tz % 8
        rows = []
        for x_half in range(2):
            parts = [flat[pl.ds(base + 128 * x_half + 8 * h, 8, stride=16), :] for h in range(2)]
            rows.append(jnp.concatenate(parts, axis=1))
        out_ref[place, tile] = jnp.concatenate(rows, axis=0).astype(BF16)


def take_entries(plan_ref, at, corner_ref, flat, kept_out, right_out, left_out):
    kept, right = plan_ref[at], plan_ref[at + 1]

    @pl.loop(0, kept)
    def _(slot):
        take_tiles(corner_ref, flat, kept_out, slot, slot)

    @pl.loop(0, right)
    def _(slot):
        take_tiles(corner_ref, flat, right_out, kept + slot, slot)

    @pl.when(plan_ref[at + 2] == 1)
    def _():
        take_tiles(corner_ref, flat, left_out, kept + right, 0)


def gather_kernel(
    column_ref, prev_ref, count_hbm, own_hbm, volume_hbm,
    plan_ref, kept_out, right_out, back_out, here_out, two_back_out,
    flat, own_left, sent, count_ref, own_ref, volume_ref, arrived,
):
    count_copy = pltpu.make_async_copy(count_hbm, count_ref, arrived.at[4])
    own_copy = pltpu.make_async_copy(own_hbm, own_ref, arrived.at[5])
    copies = [pltpu.make_async_copy(volume_hbm.at[ty], volume_ref.at[ty], arrived.at[ty]) for ty in range(TILES_Y)]
    for copy in [count_copy, own_copy] + copies:
        copy.start()
    count_copy.wait()
    write_plan(column_ref, count_ref, plan_ref, sent)
    own_copy.wait()
    flatten(volume_ref, copies, flat)
    take_entries(plan_ref, 0, own_ref, flat, kept_out, right_out, own_left)
    take_entries(plan_ref, 3, prev_ref, flat, back_out, here_out, two_back_out)
    back_out[3] = own_left[0]


def gather(column, patch_counts, corners, prev_corners, volume):
    def tiles(count):
        return jax.ShapeDtypeStruct((count, 4, 16, 256), BF16)

    return call(
        gather_kernel,
        53,
        out_shape=(jax.ShapeDtypeStruct((9,), jnp.int32), tiles(3), tiles(3), tiles(4), tiles(3), tiles(1)),
        in_specs=[SMEM_SPEC] * 2 + [pl.BlockSpec(memory_space=pltpu.HBM)] * 3,
        out_specs=(SMEM_SPEC,) + (VMEM_SPEC,) * 5,
        scratch_shapes=[
            pltpu.VMEM((TILES_Y * TILES_Z * 32, 128), F32),
            pltpu.VMEM((1, 4, 16, 256), BF16),
            pltpu.SMEM((16,), jnp.int32),
            pltpu.SMEM(patch_counts.shape, jnp.int32),
            pltpu.SMEM(corners.shape, jnp.int32),
            pltpu.VMEM((TILES_Y, TILES_Z, TILE_VOX), BF16),
            pltpu.SemaphoreType.DMA((6,)),
        ],
        name="gather",
    )(column, prev_corners, patch_counts, corners, volume)


def dot(a, b):
    return jnp.dot(a, b, preferred_element_type=F32)


def weights_kernel(first_ref, second_ref, class_ref, first_out, second_out, class_out, four, taps, turned):
    lane = lax.broadcasted_iota(jnp.int32, (32, 256), 1)
    taps[...] = jnp.zeros((32, 32), F32)
    for dx in range(3):
        for dy in range(3):
            at = 9 * dx + 3 * dy
            taps[at : at + 3, :] = first_ref[dx, dy].astype(F32)
    first = jnp.concatenate([taps[...]] * 8, axis=1)
    big = jnp.concatenate([jnp.where(lane // 32 == s, first, 0.0).astype(BF16) for s in range(8)], axis=0)
    row = lax.broadcasted_iota(jnp.int32, (256, 256), 0)
    col = lax.broadcasted_iota(jnp.int32, (256, 256), 1)
    tap = col % 32
    dx = jnp.where(tap >= 18, 2, jnp.where(tap >= 9, 1, 0))
    rest = tap - 9 * dx
    dy = jnp.where(rest >= 6, 2, jnp.where(rest >= 3, 1, 0))
    dz = rest - 3 * dy
    fits = ((row // 32) % 4 == col // 128 + dx) & (row // 128 * 2 + (row // 16) % 2 == (col // 64) % 2 + dy) & (tap < 27)
    ahead = row % 16 - (col // 32) % 2 - dz
    for j in range(6):
        spread = jnp.where(fits & (ahead == 2 * j), 1.0, 0.0).astype(BF16)
        first_out[j] = dot(spread, big).astype(BF16)

    part = lax.broadcasted_iota(jnp.int32, (32, 128), 1) // 32
    for tap in range(27):
        four[tap] = jnp.concatenate([second_ref[tap].astype(F32)] * 4, axis=1)
    for qx in range(4):
        for qy in range(4):
            for qz in range(4):
                at = ((((qy // 2 * 2 + qz // 2) * 2 + qx // 2) * 2 + qx % 2) * 2 + qy % 2) * 2 + qz % 2
                for half in range(2):
                    got = jnp.zeros((32, 128), F32)
                    for s in range(4):
                        dx, dy, dz = qx - half, qy - s // 2, qz - s % 2
                        if min(dx, dy, dz) >= 0 and max(dx, dy, dz) <= 2:
                            got = jnp.where(part == s, four[(dx * 3 + dy) * 3 + dz], got)
                    second_out[32 * at : 32 * at + 32, 128 * half : 128 * half + 128] = got.astype(BF16)

    turned[...] = jnp.zeros((128, 128), F32)
    turned[0:CLASSES, 0:CHANNELS] = class_ref[...].astype(F32)
    classes = turned[...].T
    columns = jnp.zeros((32, 256), F32)
    for k in range(CLASSES):
        columns = jnp.where(lane // 64 == k, classes[0:32, k : k + 1], columns)
    for b in range(8):
        for s in range(8):
            place = 32 * (s // 4) + 16 * (s // 2 % 2) + 2 * b + s % 2
            class_out[b, 32 * s : 32 * s + 32, :] = jnp.where(lane % 64 == place, columns, 0.0).astype(BF16)


def prepare_weights(first_kernel, second_kernel, class_weights):
    return call(
        weights_kernel,
        12,
        out_shape=(
            jax.ShapeDtypeStruct((6, 256, 256), BF16),
            jax.ShapeDtypeStruct((2048, 256), BF16),
            jax.ShapeDtypeStruct((8, 256, 256), BF16),
        ),
        in_specs=[VMEM_SPEC] * 3,
        out_specs=(VMEM_SPEC,) * 3,
        scratch_shapes=[pltpu.VMEM((27, 32, 128), F32), pltpu.VMEM((32, 32), F32), pltpu.VMEM((128, 128), F32)],
        cost_estimate=pl.CostEstimate(flops=1_000_000_000, bytes_accessed=8_000_000, transcendentals=0),
        name="weights",
    )(first_kernel, second_kernel.reshape(27, CHANNELS, CHANNELS), class_weights.T)


def fold_channels(row):
    half = row[:, :128] + row[:, 128:]
    half = half + pltpu.roll(half, 64, 1)
    half = half + pltpu.roll(half, 32, 1)
    return jnp.concatenate([half, half], axis=1)


def merge_stats(pivot, s1, s2):
    count = 4096.0
    lane_mean = pivot + s1 * (1.0 / count)
    lane_m2 = s2 - s1 * s1 * (1.0 / count)
    mean = fold_channels(lane_mean) * 0.125
    off = lane_mean - mean
    var = fold_channels(lane_m2 + count * (off * off)) * (1.0 / 32768.0)
    return mean, lax.rsqrt(var + 1e-05)


def leaky(v):
    return jnp.maximum(v, 0.01 * v)


def sum_rows(block):
    return jnp.sum(block, axis=0, keepdims=True)


def network_kernel(plan_ref, own_ref, back_ref, right_ref, here_ref, across_ref, left_ref, *refs):
    pick_ref, window_ref, first_ref, second_ref, class_ref, blend_ref = refs[:6]
    outs, (cubes, made, spread, raw, hidden_a, hidden_b, second) = refs[6:-7], refs[-7:]
    for i in range(3):
        cubes[i, 0] = own_ref[i]
        cubes[i, 1] = back_ref[i]
        cubes[3 + i, 0] = right_ref[i]
    cubes[6, 0] = back_ref[3]
    cubes[6, 1] = left_ref[0]

    @pl.when(plan_ref[8] == 0)
    def _():
        for i in range(3):
            cubes[3 + i, 1] = here_ref[i]

    @pl.when(plan_ref[8] == 1)
    def _():
        for i in range(3):
            cubes[3 + i, 1] = across_ref[i]

    spread[0] = jnp.zeros((16, 384), BF16)
    spread[17] = jnp.zeros((16, 384), BF16)
    lane = lax.broadcasted_iota(jnp.int32, (1, 256), 1)
    sy, sz = (lane % 128) // 64, (lane % 64) // 32
    y_first = (sy == 1).astype(F32)
    y_last = (sy == 0).astype(F32)
    row16 = lax.broadcasted_iota(jnp.int32, (16, 128), 0)
    lane16 = lax.broadcasted_iota(jnp.int32, (16, 128), 1) // 32

    def z_mask(bz):
        bad = ((bz == 0) & (sz == 0)) | ((bz == 16) & (sz == 1))
        return jnp.where(bad, 0.0, 1.0)

    def patch(index, carry):
        kept = plan_ref[0]
        later = jnp.where(index - kept < plan_ref[6], 3 + index - kept, 6)
        slot = jnp.where(index < kept, index, later)
        cube = jnp.concatenate(
            [jnp.concatenate([cubes[slot, tx, t] for t in range(4)], axis=1) for tx in range(2)], axis=0
        )
        moved = dot(pick_ref[...], cube)
        lists = []
        for ty in range(2):
            for quad in range(2):
                pieces = []
                for wx in range(4):
                    for tz in range(2):
                        at = (ty * 2 + tz) * 256 + quad * 128
                        pieces.append(moved[16 * wx : 16 * wx + 16, at : at + 128])
                for r in range(4):
                    joined = []
                    for tile in range(2):
                        got = None
                        for place in range(4):
                            piece = pieces[4 * tile + place]
                            turn = (32 * (place - r)) % 128
                            if turn:
                                piece = pltpu.roll(piece, turn, 1)
                            got = piece if got is None else jnp.where(lane16 == place, piece, got)
                        joined.append(got)
                    lists.append(jnp.concatenate(joined, axis=1).astype(BF16))
        rows = jnp.concatenate(lists, axis=0)
        spread[1:17] = dot(rows, window_ref[...]).astype(BF16).reshape(16, 16, 384)

        def first_plane(bz):
            lanes = slice(128 * (bz // 6), 128 * (bz // 6) + 128)
            lhs = jnp.concatenate([spread[0:17, :, lanes], spread[1:18, :, lanes]], axis=2).reshape(272, 256)
            out = dot(lhs, first_ref[bz % 6])
            raw[bz] = out
            return out

        def plane_sums(bz, out, pivot):
            d = out - pivot
            inner = d[16:256].reshape(15, 16, 256)
            edges = d[0:16] * y_first, d[256:272] * y_last
            s1 = jnp.sum(inner, axis=0) + (edges[0] + edges[1])
            s2 = jnp.sum(inner * inner, axis=0) + (edges[0] * edges[0] + edges[1] * edges[1])
            if bz in (0, 16):
                s1, s2 = s1 * z_mask(bz), s2 * z_mask(bz)
            return s1, s2

        out = first_plane(1)
        pivot = sum_rows(out[16:256]) * (1.0 / 240.0)
        s1, s2 = plane_sums(1, out, pivot)
        for bz in range(17):
            if bz != 1:
                a1, a2 = plane_sums(bz, first_plane(bz), pivot)
                s1, s2 = s1 + a1, s2 + a2
        mean, inv = merge_stats(pivot, sum_rows(s1), sum_rows(s2))

        def normalise(bz, into, place):
            scale = inv * z_mask(bz)
            for by in range(17):
                here = scale * y_first if by == 0 else scale * y_last if by == 16 else scale
                v = leaky((raw[bz, 16 * by : 16 * by + 16] - mean) * here)
                even, odd = v[:, :128], v[:, 128:]
                before = jnp.where(row16 == 0, 0.0, pltpu.roll(odd, 1, 0))
                after = jnp.where(row16 == 15, 0.0, pltpu.roll(even, 15, 0))
                into[place, by] = jnp.concatenate([before, even, odd, after], axis=1).astype(BF16)

        def second_rows(held, first, rows):
            parts = [held[first + ez, ey : ey + rows].reshape(16 * rows, 512) for ey in range(2) for ez in range(2)]
            return jnp.concatenate(parts, axis=1)

        def second_four(four, held, pivot):
            lhs = jnp.concatenate([second_rows(held, i, 16) for i in range(4)], axis=0)
            slabs = dot(lhs, second_ref[...])
            second[pl.ds(4 * four, 4)] = slabs.reshape(4, 256, 256)
            d = (slabs - pivot).reshape(64, 16, 256)
            return jnp.sum(d, axis=0), jnp.sum(d * d, axis=0)

        for bz in range(5):
            normalise(bz, hidden_a, bz)
        pivot2 = sum_rows(dot(second_rows(hidden_a, 0, 8), second_ref[...])) * (1.0 / 128.0)

        def second_loop(i, sums):
            s1, s2 = sums
            for half, (held, later) in enumerate(((hidden_a, hidden_b), (hidden_b, hidden_a))):
                a1, a2 = second_four(2 * i + half, held, pivot2)
                later[0] = held[4]
                for ahead in range(4):
                    normalise(jnp.minimum(8 * i + 4 * half + 5 + ahead, 16), later, 1 + ahead)
                s1, s2 = s1 + a1, s2 + a2
            return s1, s2

        zeros = jnp.zeros((16, 256), F32)
        s1, s2 = lax.fori_loop(0, 2, second_loop, (zeros, zeros))
        mean, inv = merge_stats(pivot2, sum_rows(s1), sum_rows(s2))

        logits = []
        for tz in range(2):
            parts, weights = [], []
            for b in range(8):
                h = leaky((second[8 * tz + b] - mean) * inv)
                top = h.astype(BF16)
                parts += [top, (h - top.astype(F32)).astype(BF16)]
                weights += [class_ref[b], class_ref[b]]
            logits.append(dot(jnp.concatenate(parts, axis=1), jnp.concatenate(weights, axis=0)))

        side = lax.broadcasted_iota(jnp.int32, (256, 128), 1) < 64
        t0, t1 = logits[0][:, 0:128], logits[0][:, 128:256]
        u0, u1 = logits[1][:, 0:128], logits[1][:, 128:256]
        l0 = jnp.where(side, t0, pltpu.roll(u0, 64, 1))
        l1 = jnp.where(side, pltpu.roll(t0, 64, 1), u0)
        l2 = jnp.where(side, t1, pltpu.roll(u1, 64, 1))
        most = jnp.maximum(jnp.maximum(l0, l1), l2)
        x0, x1, x2 = jnp.exp(l0 - most), jnp.exp(l1 - most), jnp.exp(l2 - most)
        share = blend_ref[...] / (x0 + x1 + x2)

        lane32 = lax.broadcasted_iota(jnp.int32, (64, 128), 1) // 32
        for k, x in enumerate((x0, x1)):
            w = (x * share).reshape(4, 4, 16, 128)
            sources = [w[:, r].reshape(64, 128) for r in range(4)]
            dest = []
            for q in range(4):
                got = None
                for r in range(4):
                    turn = (32 * (r - q)) % 128
                    piece = pltpu.roll(sources[r], turn, 1) if turn else sources[r]
                    got = piece if got is None else jnp.where(lane32 == r, piece, got)
                dest.append(got)
            for tx in range(2):
                for ty in range(2):
                    for h in range(2):
                        at = (2 * ty + h) * 16 + 8 * tx
                        for tz in range(2):
                            both = jnp.concatenate([dest[2 * tz][at : at + 8], dest[2 * tz + 1][at : at + 8]], axis=0)
                            rows = slice(16 * k, 16 * k + 16)
                            lanes = slice(128 * h, 128 * h + 128)
                            made[tx, slot, 2 * ty + tz, rows, lanes] = both.astype(BF16)
        return carry

    lax.fori_loop(0, plan_ref[0] + plan_ref[6] + plan_ref[7], patch, 0)
    low_out, ahead_out, right_low_out, right_up_out, left_up_out = outs
    low_out[...] = made[0, 0:3]
    ahead_out[0:3] = made[1, 0:3]
    ahead_out[3] = made[0, 6]
    right_low_out[...] = made[0, 3:6]
    right_up_out[...] = made[1, 3:6]
    left_up_out[0] = made[1, 6]


def network(plan, cubes, weights):
    def halves(count):
        return jax.ShapeDtypeStruct((count, 4, 16 * SENT, 256), BF16)

    return call(
        network_kernel,
        32,
        out_shape=(halves(3), halves(4), halves(3), halves(3), halves(1)),
        in_specs=[SMEM_SPEC] + [VMEM_SPEC] * 12,
        out_specs=(VMEM_SPEC,) * 5,
        scratch_shapes=[
            pltpu.VMEM((ENTRIES, 2, 4, 16, 256), BF16),
            pltpu.VMEM((2, ENTRIES, 4, 16 * SENT, 256), BF16),
            pltpu.VMEM((18, 16, 384), BF16),
            pltpu.VMEM((17, 272, 256), F32),
            pltpu.VMEM((5, 17, 16, 512), BF16),
            pltpu.VMEM((5, 17, 16, 512), BF16),
            pltpu.VMEM((16, 256, 256), F32),
        ],
        cost_estimate=pl.CostEstimate(flops=20_000_000_000, bytes_accessed=8_000_000, transcendentals=600_000),
        name="network",
    )(plan, *cubes, *weights)


def patch_entry(plan_ref, side, i):
    kept, right, left = [plan_ref[3 * side + j] for j in range(3)]
    if i < 3:
        return i < kept, jnp.int32(i)
    if i < 6:
        return i - 3 < right, jnp.minimum(kept + i - 3, HOME_MOST - 1)
    return left == 1, jnp.minimum(kept + right, HOME_MOST - 1)


def inverse_kernel(plan_ref, own_ref, prev_ref, parts_ref, inverse_ref, chosen_ref, chosen_parts):
    @pl.when(pl.program_id(0) == 0)
    def _():
        lane = lax.broadcasted_iota(jnp.int32, (1, 256), 1) % 64
        tiles = jnp.full((1, 256), -1, jnp.int32)
        for side, corner_ref in enumerate((own_ref, prev_ref)):
            for i in range(ENTRIES):
                live, slot = patch_entry(plan_ref, side, i)
                first = corner_ref[1, 0, slot] * TILES_Z + corner_ref[2, 0, slot]
                for t in range(4):
                    tile = jnp.where(live, first + TILES_Z * (t // 2) + t % 2, -1)
                    tiles = jnp.where(lane == 4 * (ENTRIES * side + i) + t, tile, tiles)
        same = lax.broadcasted_iota(jnp.int32, (256, 256), 0) == tiles
        hot = jnp.where(same, 1.0, 0.0).astype(BF16)
        chosen_parts[...] = hot
        chosen_ref[...] = hot[:, :128]

    weight = dot(chosen_parts[...], parts_ref[...])
    inverse_ref[...] = jnp.where(weight > 0, 1.0 / jnp.maximum(weight, 0.1), 0.0)


def inverse_weights(plan, corners, prev_corners):
    return call(
        inverse_kernel,
        12,
        grid=(4,),
        out_shape=(
            jax.ShapeDtypeStruct((TILES_Y * TILES_Z, TILE_VOX), F32),
            jax.ShapeDtypeStruct((TILES_Y * TILES_Z, 128), BF16),
        ),
        in_specs=[SMEM_SPEC] * 3 + [pl.BlockSpec((256, 1024), lambda i: (0, i))],
        out_specs=(pl.BlockSpec((256, 1024), lambda i: (0, i)), pl.BlockSpec((256, 128), lambda i: (0, 0))),
        scratch_shapes=[pltpu.VMEM((256, 256), BF16)],
        cost_estimate=pl.CostEstimate(flops=1_000_000_000, bytes_accessed=8_000_000, transcendentals=0),
        name="inverse_weights",
    )(plan, corners, prev_corners, jnp.asarray(blend_parts(), BF16))


def blend_kernel(
    plan_ref, chosen_ref, inverse_ref, low_ref, right_ref, ahead_ref, here_ref, across_ref, left_ref, out_ref, rows, stacked, staged, written
):
    for side in range(2):
        for i in range(ENTRIES):
            live, _ = patch_entry(plan_ref, side, i)
            number = 4 * (ENTRIES * side + i)
            if i < 3:
                kept_ref = (low_ref, ahead_ref)[side]
                sources = [(live, kept_ref, i)]
            elif i == 6:
                sources = [(live, left_ref, 0) if side else (live, ahead_ref, 3)]
            elif side == 0:
                sources = [(live, right_ref, i - 3)]
            else:
                starts = plan_ref[8] == 1
                sources = [
                    (live & jnp.logical_not(starts), here_ref, i - 3),
                    (live & starts, across_ref, i - 3),
                ]
            for when, part_ref, place in sources:

                @pl.when(when)
                def _():
                    for t in range(4):
                        for h in range(2):
                            piece = part_ref[place, t, :, 128 * h : 128 * h + 128]
                            at = 40 * (number + t)
                            rows[h, at : at + 16 * SENT, :] = piece.astype(F32)

            @pl.when(jnp.logical_not(live))
            def _():
                for h in range(2):
                    rows[h, 40 * number : 40 * number + 160, :] = jnp.zeros((160, 128), F32)

    blank = jnp.zeros((8, 128), F32)
    for x in range(16):
        for k in range(SENT):
            row = 16 * k + (x % 2) * 8 + x // 2
            for h in range(2):
                for pair in range(4):
                    both = [rows[h, pl.ds(640 * pair + 320 * o + row, 8, stride=40), :] if 2 * pair + o < 7 else blank for o in range(2)]
                    at = 256 * k + 128 * h
                    stacked[x, 16 * pair : 16 * pair + 16, at : at + 128] = jnp.concatenate(both, axis=0).astype(BF16)

    def part_copy(x):
        lanes = pl.ds(pl.multiple_of(256 * x, 256), 256)
        return pltpu.make_async_copy(staged.at[:, :, :, lanes], out_ref.at[:, :, :, lanes], written.at[x])

    @pl.loop(0, 16)
    def _(x):
        lanes = pl.ds(pl.multiple_of(256 * x, 256), 256)
        inv = inverse_ref[:, lanes]
        got = dot(chosen_ref[:, 0:64], stacked[x])
        p0, p1 = got[:, :256] * inv, got[:, 256:] * inv
        p2 = jnp.where(inv > 0, jnp.maximum(1.0 - p0 - p1, 0.0), 0.0)
        for k, p in enumerate((p0, p1, p2)):
            staged[:, k, :, lanes] = p.reshape(TILES_Y, TILES_Z, 256)
        part_copy(x).start()

    @pl.loop(0, 16)
    def _(x):
        part_copy(x).wait()


def blend(plan, chosen, inverse, *parts):
    shape = (TILES_Y, CLASSES, TILES_Z, TILE_VOX)
    return call(
        blend_kernel,
        28,
        out_shape=jax.ShapeDtypeStruct(shape, F32),
        in_specs=[SMEM_SPEC] + [VMEM_SPEC] * 8,
        out_specs=pl.BlockSpec(memory_space=pl.ANY),
        scratch_shapes=[
            pltpu.VMEM((2, 8 * ENTRIES * 40, 128), F32),
            pltpu.VMEM((16, 64, 256 * SENT), BF16),
            pltpu.VMEM(shape, F32),
            pltpu.SemaphoreType.DMA((16,)),
        ],
        name="blend",
    )(plan, chosen, inverse, *parts)


def passed_along(block, axis, distance):
    devices = range(lax.axis_size(axis))
    route = [(i - distance, i) for i in devices if i - distance in devices]
    return lax.ppermute(block, axis, route)


def passed_round(block, distance):
    size = lax.axis_size("bal")
    return lax.ppermute(block, "bal", [(i, (i + distance) % size) for i in range(size)])


def passed_over(block, forward):
    axes = ("slab", "bal")
    members = lax.axis_size("bal")
    pairs = [(i, i + members) for i in range(0, lax.axis_size(axes) - members, members)]
    return lax.ppermute(block, axes, pairs if forward else [(b, a) for a, b in pairs])


def local(volume, first_kernel, second_kernel, class_weights, patch_corners, patch_counts):
    axes = ("slab", "bal")
    column = lax.axis_index(axes).astype(jnp.int32)
    corners = patch_corners.transpose(2, 0, 1)
    prev_corners = passed_along(corners, axes, 1)
    laid_out = prepare_weights(first_kernel, second_kernel, class_weights)
    laid_out, prev_corners = lax.optimization_barrier((laid_out, prev_corners))
    weights = (
        jnp.asarray(select_x(), BF16),
        jnp.asarray(select_window(), BF16),
        *laid_out,
        jnp.asarray(blend_rows(), F32),
    )
    plan, own_kept, own_right, back, here, two_back = gather(column[None], patch_counts, corners, prev_corners, volume[0])
    right = passed_round(own_right, 1)
    back = passed_along(back, axes, -1)
    across = passed_over(here, False)
    left = passed_along(two_back, axes, -2)
    low, ahead, right_low, right_up, left_up = network(plan, (own_kept, back, right, here, across, left), weights)
    ahead = passed_along(ahead, axes, 1)
    right_low = passed_round(right_low, -1)
    across_up = passed_over(right_up, True)
    left_up = passed_along(left_up, axes, 2)
    corners, prev_corners, low = lax.optimization_barrier((corners, prev_corners, low))
    inverse, chosen = inverse_weights(plan, corners, prev_corners)
    out = blend(plan, chosen, inverse, low, right_low, ahead, right_up, across_up, left_up)
    return out.transpose(0, 2, 1, 3)[None]


def solution(mesh):
    return jax.shard_map(
        local,
        mesh=mesh,
        in_specs=(
            P(("slab", "bal"), None, None, None),
            P(),
            P(),
            P(),
            P(("slab", "bal"), None, None),
            P(),
        ),
        out_specs=P(("slab", "bal"), None, None, None, None),
        check_vma=False,
    )
```

```python
import jax
import jax.numpy as jnp
import numpy as np
from jax import lax
from jax.experimental import pallas as pl
from jax.experimental.pallas import tpu as pltpu
from jax.sharding import PartitionSpec as P

PATCH = 32
HALF = 16
TILE_VOX = 4096
CHANNELS = 32
CLASSES = 3
ENTRIES = 7
SENT = 2
HOME_MOST = 6
TILES_Y = 4
TILES_Z = 64
F32 = jnp.float32
BF16 = jnp.bfloat16
MIB = 1024 * 1024


def select_x():
    out = np.zeros((4, 16, 32), np.float32)
    for wx in range(4):
        for bx in range(16):
            x = 2 * bx - 1 + wx
            if 0 <= x < 32:
                out[wx, bx, x] = 1
    return out.reshape(64, 32)


def select_window():
    out = np.zeros((4, 2, 2, 16, 3, 4, 2, 16), np.float32)
    for wx in range(4):
        for ypar in range(2):
            for g in range(3):
                for zw in range(16):
                    z = 12 * g - 2 + zw
                    if 0 <= z < 32:
                        out[wx, z // 16, ypar, z % 16, g, wx, ypar, zw] = 1
    return out.reshape(256, 384)


def blend_map():
    coordinate = np.arange(PATCH, dtype=np.float32)
    square = (coordinate - np.float32(15.5)) ** 2 / np.float32(32.0)
    total = square[:, None, None] + square[None, :, None] + square[None, None, :]
    return (np.float32(0.1) + np.float32(0.9) * np.exp(-total)).astype(np.float32)


def blend_rows():
    b = blend_map().reshape(16, 2, 16, 2, 2, 16)
    return b.transpose(2, 0, 4, 1, 3, 5).reshape(256, 128)


def blend_parts():
    b = blend_map().reshape(2, 16, 2, 16, 2, 16).transpose(0, 2, 4, 1, 3, 5).reshape(2, 4, TILE_VOX)
    out = np.zeros((4, 64, TILE_VOX), np.float32)
    for side in range(2):
        for patch in range(ENTRIES):
            at = 4 * (ENTRIES * side + patch)
            rest = b[side]
            for part in range(3):
                top = rest.astype(jnp.bfloat16).astype(np.float32)
                out[part, at : at + 4] = top
                rest = rest - top
    return out.reshape(256, TILE_VOX)


def call(kernel, vmem, **options):
    params = pltpu.CompilerParams(vmem_limit_bytes=vmem * MIB)
    return pl.pallas_call(kernel, compiler_params=params, **options)


SMEM_SPEC = pl.BlockSpec(memory_space=pltpu.SMEM)
VMEM_SPEC = pl.BlockSpec(memory_space=pltpu.VMEM)


def write_plan(column_ref, count_ref, plan_ref, sent):
    column = column_ref[0]

    def group_plan(group, at):
        heavy = jnp.int32(0)
        for i in (3, 2, 1, 0):
            heavy = jnp.where(count_ref[4 * group + i] == HOME_MOST, i, heavy)
        place = [(heavy + k) % 4 for k in range(4)]
        count = [count_ref[4 * group + place[k]] for k in range(4)]
        left = [jnp.where((count[1] >= 4) & (heavy >= 1), 1, 0), 0, 0, 0]
        right = []
        coming = 0
        for k in range(4):
            load = count[k] + coming - left[k]
            if k == 3:
                load = load + left[0]
                left[3] = jnp.where((load > 3) & (place[3] >= 1), 1, 0)
                load = load - left[3]
            out = jnp.clip(load - 3, 0, jnp.minimum(count[k] - left[k], 3))
            right.append(out)
            coming = out
        for k in range(4):
            sent[at + place[k]] = right[k]
            sent[at + 4 + place[k]] = left[k]

    def column_plan(where, at, out):
        me = where % 4
        right, left = sent[at + me], sent[at + 4 + me]
        plan_ref[out] = count_ref[where] - right - left
        plan_ref[out + 1] = right
        plan_ref[out + 2] = left

    group_plan(column // 4, 0)
    column_plan(column, 0, 0)
    me = column % 4
    plan_ref[6] = sent[(me + 3) % 4]
    plan_ref[7] = jnp.where(me == 3, 0, sent[4 + (me + 1) % 4])
    plan_ref[8] = jnp.where(me == 0, 1, 0)
    before = jnp.maximum(column - 1, 0)
    group_plan(before // 4, 8)
    column_plan(before, 8, 3)

    @pl.when(column == 0)
    def _():
        for i in range(3):
            plan_ref[3 + i] = 0


def flatten(volume_ref, copies, flat):
    for ty in range(TILES_Y):
        copies[ty].wait()
        for group in range(TILES_Z // 16):
            for lane_tile in range(32):
                block = volume_ref[ty, 16 * group : 16 * group + 16, 128 * lane_tile : 128 * lane_tile + 128].astype(F32)
                for half in range(2):
                    start = ((ty * 8 + 2 * group + half) * 32 + lane_tile) * 8
                    flat[start : start + 8, :] = block[8 * half : 8 * half + 8]


def take_tiles(corner_ref, flat, out_ref, slot, place):
    for tile in range(4):
        ty = corner_ref[1, 0, slot] + tile // 2
        tz = corner_ref[2, 0, slot] + tile % 2
        base = (ty * 8 + tz // 8) * 256 + tz % 8
        rows = []
        for x_half in range(2):
            parts = [flat[pl.ds(base + 128 * x_half + 8 * h, 8, stride=16), :] for h in range(2)]
            rows.append(jnp.concatenate(parts, axis=1))
        out_ref[place, tile] = jnp.concatenate(rows, axis=0).astype(BF16)


def take_entries(plan_ref, at, corner_ref, flat, kept_out, right_out, left_out):
    kept, right = plan_ref[at], plan_ref[at + 1]

    @pl.loop(0, kept)
    def _(slot):
        take_tiles(corner_ref, flat, kept_out, slot, slot)

    @pl.loop(0, right)
    def _(slot):
        take_tiles(corner_ref, flat, right_out, kept + slot, slot)

    @pl.when(plan_ref[at + 2] == 1)
    def _():
        take_tiles(corner_ref, flat, left_out, kept + right, 0)


def gather_kernel(
    plan_ref, own_ref, prev_ref, volume_hbm,
    kept_out, right_out, back_out, here_out, two_back_out,
    flat, own_left, volume_ref, arrived,
):
    copies = [pltpu.make_async_copy(volume_hbm.at[ty], volume_ref.at[ty], arrived.at[ty]) for ty in range(TILES_Y)]
    for copy in copies:
        copy.start()
    flatten(volume_ref, copies, flat)
    take_entries(plan_ref, 0, own_ref, flat, kept_out, right_out, own_left)
    take_entries(plan_ref, 3, prev_ref, flat, back_out, here_out, two_back_out)
    back_out[3] = own_left[0]


def gather(plan, corners, prev_corners, volume):
    def tiles(count):
        return jax.ShapeDtypeStruct((count, 4, 16, 256), BF16)

    return call(
        gather_kernel,
        53,
        out_shape=(tiles(3), tiles(3), tiles(4), tiles(3), tiles(1)),
        in_specs=[SMEM_SPEC] * 3 + [pl.BlockSpec(memory_space=pltpu.HBM)],
        out_specs=(VMEM_SPEC,) * 5,
        scratch_shapes=[
            pltpu.VMEM((TILES_Y * TILES_Z * 32, 128), F32),
            pltpu.VMEM((1, 4, 16, 256), BF16),
            pltpu.VMEM((TILES_Y, TILES_Z, TILE_VOX), BF16),
            pltpu.SemaphoreType.DMA((TILES_Y,)),
        ],
        name="gather",
    )(plan, corners, prev_corners, volume)


def dot(a, b):
    return jnp.dot(a, b, preferred_element_type=F32)


def weights_kernel(
    column_ref, count_ref, corner_ref, first_ref, second_ref, class_ref,
    plan_ref, corner_out, first_out, second_out, class_out, four, taps, turned, sent,
):
    write_plan(column_ref, count_ref, plan_ref, sent)
    for i in range(3):
        for slot in range(HOME_MOST):
            corner_out[i, 0, slot] = corner_ref[i, 0, slot]
    lane = lax.broadcasted_iota(jnp.int32, (32, 256), 1)
    taps[...] = jnp.zeros((32, 32), F32)
    for dx in range(3):
        for dy in range(3):
            at = 9 * dx + 3 * dy
            taps[at : at + 3, :] = first_ref[dx, dy].astype(F32)
    first = jnp.concatenate([taps[...]] * 8, axis=1)
    big = jnp.concatenate([jnp.where(lane // 32 == s, first, 0.0).astype(BF16) for s in range(8)], axis=0)
    row = lax.broadcasted_iota(jnp.int32, (256, 256), 0)
    col = lax.broadcasted_iota(jnp.int32, (256, 256), 1)
    tap = col % 32
    dx = jnp.where(tap >= 18, 2, jnp.where(tap >= 9, 1, 0))
    rest = tap - 9 * dx
    dy = jnp.where(rest >= 6, 2, jnp.where(rest >= 3, 1, 0))
    dz = rest - 3 * dy
    fits = ((row // 32) % 4 == col // 128 + dx) & (row // 128 * 2 + (row // 16) % 2 == (col // 64) % 2 + dy) & (tap < 27)
    ahead = row % 16 - (col // 32) % 2 - dz
    for j in range(6):
        spread = jnp.where(fits & (ahead == 2 * j), 1.0, 0.0).astype(BF16)
        first_out[j] = dot(spread, big).astype(BF16)

    part = lax.broadcasted_iota(jnp.int32, (32, 128), 1) // 32
    for tap in range(27):
        four[tap] = jnp.concatenate([second_ref[tap].astype(F32)] * 4, axis=1)
    for qx in range(4):
        for qy in range(4):
            for qz in range(4):
                at = ((((qy // 2 * 2 + qz // 2) * 2 + qx // 2) * 2 + qx % 2) * 2 + qy % 2) * 2 + qz % 2
                for half in range(2):
                    got = jnp.zeros((32, 128), F32)
                    for s in range(4):
                        dx, dy, dz = qx - half, qy - s // 2, qz - s % 2
                        if min(dx, dy, dz) >= 0 and max(dx, dy, dz) <= 2:
                            got = jnp.where(part == s, four[(dx * 3 + dy) * 3 + dz], got)
                    second_out[32 * at : 32 * at + 32, 128 * half : 128 * half + 128] = got.astype(BF16)

    turned[...] = jnp.zeros((128, 128), F32)
    turned[0:CLASSES, 0:CHANNELS] = class_ref[...].astype(F32)
    classes = turned[...].T
    columns = jnp.zeros((32, 256), F32)
    for k in range(CLASSES):
        columns = jnp.where(lane // 64 == k, classes[0:32, k : k + 1], columns)
    for b in range(8):
        for s in range(8):
            place = 32 * (s // 4) + 16 * (s // 2 % 2) + 2 * b + s % 2
            class_out[b, 32 * s : 32 * s + 32, :] = jnp.where(lane % 64 == place, columns, 0.0).astype(BF16)


def prepare(column, patch_counts, corners, first_kernel, second_kernel, class_weights):
    return call(
        weights_kernel,
        12,
        out_shape=(
            jax.ShapeDtypeStruct((9,), jnp.int32),
            jax.ShapeDtypeStruct(corners.shape, jnp.int32),
            jax.ShapeDtypeStruct((6, 256, 256), BF16),
            jax.ShapeDtypeStruct((2048, 256), BF16),
            jax.ShapeDtypeStruct((8, 256, 256), BF16),
        ),
        in_specs=[SMEM_SPEC] * 3 + [VMEM_SPEC] * 3,
        out_specs=(SMEM_SPEC,) * 2 + (VMEM_SPEC,) * 3,
        scratch_shapes=[
            pltpu.VMEM((27, 32, 128), F32),
            pltpu.VMEM((32, 32), F32),
            pltpu.VMEM((128, 128), F32),
            pltpu.SMEM((16,), jnp.int32),
        ],
        cost_estimate=pl.CostEstimate(flops=1_000_000_000, bytes_accessed=8_000_000, transcendentals=0),
        name="weights",
    )(column, patch_counts, corners, first_kernel, second_kernel.reshape(27, CHANNELS, CHANNELS), class_weights.T)


def fold_channels(row):
    half = row[:, :128] + row[:, 128:]
    half = half + pltpu.roll(half, 64, 1)
    half = half + pltpu.roll(half, 32, 1)
    return jnp.concatenate([half, half], axis=1)


def merge_stats(pivot, s1, s2):
    count = 4096.0
    lane_mean = pivot + s1 * (1.0 / count)
    lane_m2 = s2 - s1 * s1 * (1.0 / count)
    mean = fold_channels(lane_mean) * 0.125
    off = lane_mean - mean
    var = fold_channels(lane_m2 + count * (off * off)) * (1.0 / 32768.0)
    return mean, lax.rsqrt(var + 1e-05)


def leaky(v):
    return jnp.maximum(v, 0.01 * v)


def sum_rows(block):
    return jnp.sum(block, axis=0, keepdims=True)


def network_kernel(plan_ref, own_ref, back_ref, right_ref, here_ref, across_ref, left_ref, *refs):
    pick_ref, window_ref, first_ref, second_ref, class_ref, blend_ref = refs[:6]
    outs, (cubes, made, spread, raw, hidden_a, hidden_b, second) = refs[6:-7], refs[-7:]
    for i in range(3):
        cubes[i, 0] = own_ref[i]
        cubes[i, 1] = back_ref[i]
        cubes[3 + i, 0] = right_ref[i]
    cubes[6, 0] = back_ref[3]
    cubes[6, 1] = left_ref[0]

    @pl.when(plan_ref[8] == 0)
    def _():
        for i in range(3):
            cubes[3 + i, 1] = here_ref[i]

    @pl.when(plan_ref[8] == 1)
    def _():
        for i in range(3):
            cubes[3 + i, 1] = across_ref[i]

    spread[0] = jnp.zeros((16, 384), BF16)
    spread[17] = jnp.zeros((16, 384), BF16)
    lane = lax.broadcasted_iota(jnp.int32, (1, 256), 1)
    sy, sz = (lane % 128) // 64, (lane % 64) // 32
    y_first = (sy == 1).astype(F32)
    y_last = (sy == 0).astype(F32)
    row16 = lax.broadcasted_iota(jnp.int32, (16, 128), 0)
    lane16 = lax.broadcasted_iota(jnp.int32, (16, 128), 1) // 32

    def z_mask(bz):
        bad = ((bz == 0) & (sz == 0)) | ((bz == 16) & (sz == 1))
        return jnp.where(bad, 0.0, 1.0)

    def patch(index, carry):
        kept = plan_ref[0]
        later = jnp.where(index - kept < plan_ref[6], 3 + index - kept, 6)
        slot = jnp.where(index < kept, index, later)
        cube = jnp.concatenate(
            [jnp.concatenate([cubes[slot, tx, t] for t in range(4)], axis=1) for tx in range(2)], axis=0
        )
        moved = dot(pick_ref[...], cube)
        lists = []
        for ty in range(2):
            for quad in range(2):
                pieces = []
                for wx in range(4):
                    for tz in range(2):
                        at = (ty * 2 + tz) * 256 + quad * 128
                        pieces.append(moved[16 * wx : 16 * wx + 16, at : at + 128])
                for r in range(4):
                    joined = []
                    for tile in range(2):
                        got = None
                        for place in range(4):
                            piece = pieces[4 * tile + place]
                            turn = (32 * (place - r)) % 128
                            if turn:
                                piece = pltpu.roll(piece, turn, 1)
                            got = piece if got is None else jnp.where(lane16 == place, piece, got)
                        joined.append(got)
                    lists.append(jnp.concatenate(joined, axis=1).astype(BF16))
        rows = jnp.concatenate(lists, axis=0)
        spread[1:17] = dot(rows, window_ref[...]).astype(BF16).reshape(16, 16, 384)

        def first_plane(bz):
            lanes = slice(128 * (bz // 6), 128 * (bz // 6) + 128)
            lhs = jnp.concatenate([spread[0:17, :, lanes], spread[1:18, :, lanes]], axis=2).reshape(272, 256)
            out = dot(lhs, first_ref[bz % 6])
            raw[bz] = out
            return out

        def plane_sums(bz, out, pivot):
            d = out - pivot
            inner = d[16:256].reshape(15, 16, 256)
            edges = d[0:16] * y_first, d[256:272] * y_last
            s1 = jnp.sum(inner, axis=0) + (edges[0] + edges[1])
            s2 = jnp.sum(inner * inner, axis=0) + (edges[0] * edges[0] + edges[1] * edges[1])
            if bz in (0, 16):
                s1, s2 = s1 * z_mask(bz), s2 * z_mask(bz)
            return s1, s2

        out = first_plane(1)
        pivot = sum_rows(out[16:256]) * (1.0 / 240.0)
        s1, s2 = plane_sums(1, out, pivot)
        for bz in range(17):
            if bz != 1:
                a1, a2 = plane_sums(bz, first_plane(bz), pivot)
                s1, s2 = s1 + a1, s2 + a2
        mean, inv = merge_stats(pivot, sum_rows(s1), sum_rows(s2))

        def normalise(bz, into, place):
            scale = inv * z_mask(bz)
            for by in range(17):
                here = scale * y_first if by == 0 else scale * y_last if by == 16 else scale
                v = leaky((raw[bz, 16 * by : 16 * by + 16] - mean) * here)
                even, odd = v[:, :128], v[:, 128:]
                before = jnp.where(row16 == 0, 0.0, pltpu.roll(odd, 1, 0))
                after = jnp.where(row16 == 15, 0.0, pltpu.roll(even, 15, 0))
                into[place, by] = jnp.concatenate([before, even, odd, after], axis=1).astype(BF16)

        def second_rows(held, first, rows):
            parts = [held[first + ez, ey : ey + rows].reshape(16 * rows, 512) for ey in range(2) for ez in range(2)]
            return jnp.concatenate(parts, axis=1)

        def second_four(four, held, pivot):
            lhs = jnp.concatenate([second_rows(held, i, 16) for i in range(4)], axis=0)
            slabs = dot(lhs, second_ref[...])
            second[pl.ds(4 * four, 4)] = slabs.reshape(4, 256, 256)
            d = (slabs - pivot).reshape(64, 16, 256)
            return jnp.sum(d, axis=0), jnp.sum(d * d, axis=0)

        for bz in range(5):
            normalise(bz, hidden_a, bz)
        pivot2 = sum_rows(dot(second_rows(hidden_a, 0, 8), second_ref[...])) * (1.0 / 128.0)

        def second_loop(i, sums):
            s1, s2 = sums
            for half, (held, later) in enumerate(((hidden_a, hidden_b), (hidden_b, hidden_a))):
                a1, a2 = second_four(2 * i + half, held, pivot2)
                later[0] = held[4]
                for ahead in range(4):
                    normalise(jnp.minimum(8 * i + 4 * half + 5 + ahead, 16), later, 1 + ahead)
                s1, s2 = s1 + a1, s2 + a2
            return s1, s2

        zeros = jnp.zeros((16, 256), F32)
        s1, s2 = lax.fori_loop(0, 2, second_loop, (zeros, zeros))
        mean, inv = merge_stats(pivot2, sum_rows(s1), sum_rows(s2))

        logits = []
        for tz in range(2):
            parts, weights = [], []
            for b in range(8):
                h = leaky((second[8 * tz + b] - mean) * inv)
                top = h.astype(BF16)
                parts += [top, (h - top.astype(F32)).astype(BF16)]
                weights += [class_ref[b], class_ref[b]]
            logits.append(dot(jnp.concatenate(parts, axis=1), jnp.concatenate(weights, axis=0)))

        side = lax.broadcasted_iota(jnp.int32, (256, 128), 1) < 64
        t0, t1 = logits[0][:, 0:128], logits[0][:, 128:256]
        u0, u1 = logits[1][:, 0:128], logits[1][:, 128:256]
        l0 = jnp.where(side, t0, pltpu.roll(u0, 64, 1))
        l1 = jnp.where(side, pltpu.roll(t0, 64, 1), u0)
        l2 = jnp.where(side, t1, pltpu.roll(u1, 64, 1))
        most = jnp.maximum(jnp.maximum(l0, l1), l2)
        x0, x1, x2 = jnp.exp(l0 - most), jnp.exp(l1 - most), jnp.exp(l2 - most)
        share = blend_ref[...] / (x0 + x1 + x2)

        lane32 = lax.broadcasted_iota(jnp.int32, (64, 128), 1) // 32
        for k, x in enumerate((x0, x1)):
            w = (x * share).reshape(4, 4, 16, 128)
            sources = [w[:, r].reshape(64, 128) for r in range(4)]
            dest = []
            for q in range(4):
                got = None
                for r in range(4):
                    turn = (32 * (r - q)) % 128
                    piece = pltpu.roll(sources[r], turn, 1) if turn else sources[r]
                    got = piece if got is None else jnp.where(lane32 == r, piece, got)
                dest.append(got)
            for tx in range(2):
                for ty in range(2):
                    for h in range(2):
                        at = (2 * ty + h) * 16 + 8 * tx
                        for tz in range(2):
                            both = jnp.concatenate([dest[2 * tz][at : at + 8], dest[2 * tz + 1][at : at + 8]], axis=0)
                            rows = slice(16 * k, 16 * k + 16)
                            lanes = slice(128 * h, 128 * h + 128)
                            made[tx, slot, 2 * ty + tz, rows, lanes] = both.astype(BF16)
        return carry

    lax.fori_loop(0, plan_ref[0] + plan_ref[6] + plan_ref[7], patch, 0)
    low_out, ahead_out, right_low_out, right_up_out, left_up_out = outs
    low_out[...] = made[0, 0:3]
    ahead_out[0:3] = made[1, 0:3]
    ahead_out[3] = made[0, 6]
    right_low_out[...] = made[0, 3:6]
    right_up_out[...] = made[1, 3:6]
    left_up_out[0] = made[1, 6]


def network(plan, cubes, weights):
    def halves(count):
        return jax.ShapeDtypeStruct((count, 4, 16 * SENT, 256), BF16)

    return call(
        network_kernel,
        32,
        out_shape=(halves(3), halves(4), halves(3), halves(3), halves(1)),
        in_specs=[SMEM_SPEC] + [VMEM_SPEC] * 12,
        out_specs=(VMEM_SPEC,) * 5,
        scratch_shapes=[
            pltpu.VMEM((ENTRIES, 2, 4, 16, 256), BF16),
            pltpu.VMEM((2, ENTRIES, 4, 16 * SENT, 256), BF16),
            pltpu.VMEM((18, 16, 384), BF16),
            pltpu.VMEM((17, 272, 256), F32),
            pltpu.VMEM((5, 17, 16, 512), BF16),
            pltpu.VMEM((5, 17, 16, 512), BF16),
            pltpu.VMEM((16, 256, 256), F32),
        ],
        cost_estimate=pl.CostEstimate(flops=20_000_000_000, bytes_accessed=8_000_000, transcendentals=600_000),
        name="network",
    )(plan, *cubes, *weights)


def patch_entry(plan_ref, side, i):
    kept, right, left = [plan_ref[3 * side + j] for j in range(3)]
    if i < 3:
        return i < kept, jnp.int32(i)
    if i < 6:
        return i - 3 < right, jnp.minimum(kept + i - 3, HOME_MOST - 1)
    return left == 1, jnp.minimum(kept + right, HOME_MOST - 1)


def inverse_kernel(plan_ref, own_ref, prev_ref, parts_ref, inverse_ref, chosen_ref, chosen_parts):
    @pl.when(pl.program_id(0) == 0)
    def _():
        lane = lax.broadcasted_iota(jnp.int32, (1, 256), 1) % 64
        tiles = jnp.full((1, 256), -1, jnp.int32)
        for side, corner_ref in enumerate((own_ref, prev_ref)):
            for i in range(ENTRIES):
                live, slot = patch_entry(plan_ref, side, i)
                first = corner_ref[1, 0, slot] * TILES_Z + corner_ref[2, 0, slot]
                for t in range(4):
                    tile = jnp.where(live, first + TILES_Z * (t // 2) + t % 2, -1)
                    tiles = jnp.where(lane == 4 * (ENTRIES * side + i) + t, tile, tiles)
        same = lax.broadcasted_iota(jnp.int32, (256, 256), 0) == tiles
        hot = jnp.where(same, 1.0, 0.0).astype(BF16)
        chosen_parts[...] = hot
        chosen_ref[...] = hot[:, :128]

    weight = dot(chosen_parts[...], parts_ref[...])
    inverse_ref[...] = jnp.where(weight > 0, 1.0 / jnp.maximum(weight, 0.1), 0.0)


def inverse_weights(plan, corners, prev_corners):
    return call(
        inverse_kernel,
        12,
        grid=(4,),
        out_shape=(
            jax.ShapeDtypeStruct((TILES_Y * TILES_Z, TILE_VOX), F32),
            jax.ShapeDtypeStruct((TILES_Y * TILES_Z, 128), BF16),
        ),
        in_specs=[SMEM_SPEC] * 3 + [pl.BlockSpec((256, 1024), lambda i: (0, i))],
        out_specs=(pl.BlockSpec((256, 1024), lambda i: (0, i)), pl.BlockSpec((256, 128), lambda i: (0, 0))),
        scratch_shapes=[pltpu.VMEM((256, 256), BF16)],
        cost_estimate=pl.CostEstimate(flops=1_000_000_000, bytes_accessed=8_000_000, transcendentals=0),
        name="inverse_weights",
    )(plan, corners, prev_corners, jnp.asarray(blend_parts(), BF16))


def blend_kernel(
    plan_ref, chosen_ref, inverse_ref, low_ref, right_ref, ahead_ref, here_ref, across_ref, left_ref, out_ref, rows, stacked, staged, written
):
    for side in range(2):
        for i in range(ENTRIES):
            live, _ = patch_entry(plan_ref, side, i)
            number = 4 * (ENTRIES * side + i)
            if i < 3:
                kept_ref = (low_ref, ahead_ref)[side]
                sources = [(live, kept_ref, i)]
            elif i == 6:
                sources = [(live, left_ref, 0) if side else (live, ahead_ref, 3)]
            elif side == 0:
                sources = [(live, right_ref, i - 3)]
            else:
                starts = plan_ref[8] == 1
                sources = [
                    (live & jnp.logical_not(starts), here_ref, i - 3),
                    (live & starts, across_ref, i - 3),
                ]
            for when, part_ref, place in sources:

                @pl.when(when)
                def _():
                    for t in range(4):
                        for h in range(2):
                            piece = part_ref[place, t, :, 128 * h : 128 * h + 128]
                            at = 40 * (number + t)
                            rows[h, at : at + 16 * SENT, :] = piece.astype(F32)

            @pl.when(jnp.logical_not(live))
            def _():
                for h in range(2):
                    rows[h, 40 * number : 40 * number + 160, :] = jnp.zeros((160, 128), F32)

    blank = jnp.zeros((8, 128), F32)
    for x in range(16):
        for k in range(SENT):
            row = 16 * k + (x % 2) * 8 + x // 2
            for h in range(2):
                for pair in range(4):
                    both = [rows[h, pl.ds(640 * pair + 320 * o + row, 8, stride=40), :] if 2 * pair + o < 7 else blank for o in range(2)]
                    at = 256 * k + 128 * h
                    stacked[x, 16 * pair : 16 * pair + 16, at : at + 128] = jnp.concatenate(both, axis=0).astype(BF16)

    def part_copy(x):
        lanes = pl.ds(pl.multiple_of(256 * x, 256), 256)
        return pltpu.make_async_copy(staged.at[:, :, :, lanes], out_ref.at[:, :, :, lanes], written.at[x])

    @pl.loop(0, 16)
    def _(x):
        lanes = pl.ds(pl.multiple_of(256 * x, 256), 256)
        inv = inverse_ref[:, lanes]
        got = dot(chosen_ref[:, 0:64], stacked[x])
        p0, p1 = got[:, :256] * inv, got[:, 256:] * inv
        p2 = jnp.where(inv > 0, jnp.maximum(1.0 - p0 - p1, 0.0), 0.0)
        for k, p in enumerate((p0, p1, p2)):
            staged[:, k, :, lanes] = p.reshape(TILES_Y, TILES_Z, 256)
        part_copy(x).start()

    @pl.loop(0, 16)
    def _(x):
        part_copy(x).wait()


def blend(plan, chosen, inverse, *parts):
    shape = (TILES_Y, CLASSES, TILES_Z, TILE_VOX)
    return call(
        blend_kernel,
        28,
        out_shape=jax.ShapeDtypeStruct(shape, F32),
        in_specs=[SMEM_SPEC] + [VMEM_SPEC] * 8,
        out_specs=pl.BlockSpec(memory_space=pl.ANY),
        scratch_shapes=[
            pltpu.VMEM((2, 8 * ENTRIES * 40, 128), F32),
            pltpu.VMEM((16, 64, 256 * SENT), BF16),
            pltpu.VMEM(shape, F32),
            pltpu.SemaphoreType.DMA((16,)),
        ],
        name="blend",
    )(plan, chosen, inverse, *parts)


def passed_along(block, axis, distance):
    devices = range(lax.axis_size(axis))
    route = [(i - distance, i) for i in devices if i - distance in devices]
    return lax.ppermute(block, axis, route)


def passed_round(block, distance):
    size = lax.axis_size("bal")
    return lax.ppermute(block, "bal", [(i, (i + distance) % size) for i in range(size)])


def passed_over(block, forward):
    axes = ("slab", "bal")
    members = lax.axis_size("bal")
    pairs = [(i, i + members) for i in range(0, lax.axis_size(axes) - members, members)]
    return lax.ppermute(block, axes, pairs if forward else [(b, a) for a, b in pairs])


def local(volume, first_kernel, second_kernel, class_weights, patch_corners, patch_counts):
    axes = ("slab", "bal")
    column = lax.axis_index(axes).astype(jnp.int32)
    corners = patch_corners.transpose(2, 0, 1)
    prev_corners = passed_along(corners, axes, 1)
    prepared = prepare(column[None], patch_counts, corners, first_kernel, second_kernel, class_weights)
    (plan, corners, *laid_out), prev_corners = lax.optimization_barrier((prepared, prev_corners))
    weights = (
        jnp.asarray(select_x(), BF16),
        jnp.asarray(select_window(), BF16),
        *laid_out,
        jnp.asarray(blend_rows(), F32),
    )
    own_kept, own_right, back, here, two_back = gather(plan, corners, prev_corners, volume[0])
    right = passed_round(own_right, 1)
    back = passed_along(back, axes, -1)
    across = passed_over(here, False)
    left = passed_along(two_back, axes, -2)
    low, ahead, right_low, right_up, left_up = network(plan, (own_kept, back, right, here, across, left), weights)
    ahead = passed_along(ahead, axes, 1)
    right_low = passed_round(right_low, -1)
    across_up = passed_over(right_up, True)
    left_up = passed_along(left_up, axes, 2)
    corners, prev_corners, low = lax.optimization_barrier((corners, prev_corners, low))
    inverse, chosen = inverse_weights(plan, corners, prev_corners)
    out = blend(plan, chosen, inverse, low, right_low, ahead, right_up, across_up, left_up)
    return out.transpose(0, 2, 1, 3)[None]


def solution(mesh):
    return jax.shard_map(
        local,
        mesh=mesh,
        in_specs=(
            P(("slab", "bal"), None, None, None),
            P(),
            P(),
            P(),
            P(("slab", "bal"), None, None),
            P(),
        ),
        out_specs=P(("slab", "bal"), None, None, None, None),
        check_vma=False,
    )
```
